128 devices in a mesh: phi: 8 (over z, core), theta: 8 (over x, y_hi), row: 2 (over y_lo).
Axes of the slice: x: 4, y: 4 (y_hi: 2, y_lo: 2; y = y_hi * 2 + y_lo), z: 4, core: 2. Of those that a mesh axis runs over, the one named last changes fastest.
Arguments:
- test_fields: float32 [27, 8, 256, 2048], P(None, 'row', 'theta', 'phi'), may hold values from -6 to 6
- velocity: float32 [3, 8, 256, 2048], P(None, 'row', 'theta', 'phi'), may hold values from -6 to 6
- kept: int32 [256], P('theta'), may hold values from 64 to 512, as said below
Outputs:
- result: float32 [27, 8, 256, 2048], P(None, 'row', 'theta', 'phi')
- emf: float32 [27, 8, 256], P(None, 'row', ('theta', 'phi'))
The draws below stay inside these ranges and needn't reach their ends.
Inputs may be any that keep to these rules, and one draw needn't show every extreme that they name: `kept`: row 0 keeps 512 modes.
All inputs are finite; a program needn't handle non-finite values.
Results may differ from the reference program's by a relative error of at most 0.000094.
Values sent between devices are 32-bit elements; how exact they have to be, the bound alone decides.
A program may use at most 128 MiB of HBM per device.

```python
import math
import jax
import jax.numpy as jnp
from jax import lax

NPHI = 2048
FIELDS = 27
MMAX = 512
NR = 8
NT = 256


def draw_kept(key, part):
    key = jax.random.fold_in(key, 7)
    values = jax.random.randint(key, (NT,), MMAX // 8, MMAX + 1, dtype=jnp.int32)
    return values.at[0].set(MMAX)


def block_levels(key, dims, split, least, high):
    gain, own = 1.0, jax.random.fold_in(key, 6)
    for position, shards_of in split:
        steps = jnp.exp(jax.random.uniform(jax.random.fold_in(own, position), (shards_of,), jnp.float32, least / len(split), high / len(split)))
        gain = gain * jnp.repeat(steps, dims[position] // shards_of).reshape([-1 if axis == position else 1 for axis in range(len(dims))])
    return gain


def centred(rng, extent, spread, most, pieces=(), kind=jnp.bfloat16):
    values = jax.random.normal(rng, extent, jnp.float32) * spread
    if len(pieces) > 0:
        values = block_levels(rng, extent, pieces, -0.22, 0.18) * values
    return jnp.clip(values, min=-most, max=most).astype(kind)


def setup_inputs(seed: int = 0) -> dict:
    splits = jax.random.split(jax.random.key(seed), 4)
    test_fields = centred(splits[0], (FIELDS, NR, NT, NPHI), 1.0, 6.0, ((1, 2), (2, 8), (3, 8)), jnp.float32)
    velocity = centred(splits[1], (3, NR, NT, NPHI), 1.0, 6.0, ((1, 2), (2, 8), (3, 8)), jnp.float32)
    kept = draw_kept(jax.random.fold_in(splits[3], 71), 0)
    return dict(test_fields=test_fields, velocity=velocity, kept=kept)


inner_radius = 0.7
shell_depth = 0.3
coef_radial = 0.2
coef_polar = 0.1
source_step = 0.5


def fourier_tables(first_cell, cell_total):
    mode_index = jnp.arange(MMAX, dtype=jnp.int32)[:, None]
    cell_index = (first_cell + jnp.arange(cell_total, dtype=jnp.int32))[None, :]
    angles = ((mode_index * cell_index) % NPHI).astype(jnp.float32) * jnp.float32(2.0 * math.pi / NPHI)
    return jnp.cos(angles), jnp.sin(angles)


def mode_weights(counts):
    mode_index = jnp.arange(MMAX, dtype=jnp.int32)[None, :]
    mode_scale = jnp.where(mode_index == 0, jnp.float32(1.0 / NPHI), jnp.float32(2.0 / NPHI))
    return jnp.where(mode_index < counts[:, None], mode_scale, jnp.float32(0.0))


def geometry(radial_index, polar_index, radial_total, polar_total):
    cell_width = shell_depth / radial_total
    radius = inner_radius + cell_width * (radial_index.astype(jnp.float32) + 0.5)
    outward = ((radius + 0.5 * cell_width) / radius) ** 2
    inward = ((radius - 0.5 * cell_width) / radius) ** 2
    metric = (1.0 / radius) ** 2
    angle_step = math.pi / polar_total
    polar_angle = angle_step * (polar_index.astype(jnp.float32) + 0.5)
    north_side = jnp.sin(polar_angle - 0.5 * angle_step) / jnp.sin(polar_angle)
    south_side = jnp.sin(polar_angle + 0.5 * angle_step) / jnp.sin(polar_angle)
    polar_rows = ((2 * polar_index + 1) * 3 < polar_total) | ((2 * (polar_total - 1 - polar_index) + 1) * 3 < polar_total)
    profiles = jnp.stack([jnp.ones_like(polar_angle), jnp.cos(polar_angle), jnp.sin(polar_angle)])
    return outward, inward, metric, north_side, south_side, polar_rows, profiles


def diffuse(padded, outward, inward, metric, north_side, south_side):
    center = padded[:, 1:-1, 1:-1]
    radial_part = outward[:, None, None] * (padded[:, 2:, 1:-1] - center) - inward[:, None, None] * (center - padded[:, :-2, 1:-1])
    polar_part = south_side[None, :, None] * (padded[:, 1:-1, 2:] - center) - north_side[None, :, None] * (center - padded[:, 1:-1, :-2])
    return coef_radial * radial_part + coef_polar * metric[:, None, None] * polar_part


def sources(velocity, profiles):
    vel_radial, vel_polar, vel_azimuth = velocity[0], velocity[1], velocity[2]
    zero_part = jnp.zeros_like(vel_radial)
    crossed = jnp.stack([
        jnp.stack([zero_part, vel_azimuth, -vel_polar]),
        jnp.stack([-vel_azimuth, zero_part, vel_radial]),
        jnp.stack([vel_polar, -vel_radial, zero_part]),
    ])
    source = crossed[:, None] * profiles[None, :, None, None, :, None]
    return source.reshape((27,) + vel_radial.shape)


def emf_terms(velocity, field_data):
    grouped = field_data.reshape((9, 3) + field_data.shape[1:])
    first_term = velocity[1] * grouped[:, 2] - velocity[2] * grouped[:, 1]
    second_term = velocity[2] * grouped[:, 0] - velocity[0] * grouped[:, 2]
    third_term = velocity[0] * grouped[:, 1] - velocity[1] * grouped[:, 0]
    crossed = jnp.stack([first_term, second_term, third_term], axis=1)
    return jnp.sum(crossed, axis=-1).reshape((27,) + field_data.shape[1:3])


def reference(test_fields, velocity, kept):
    radial_total, polar_total = test_fields.shape[1], test_fields.shape[2]
    outward, inward, metric, north_side, south_side, polar_rows, profiles = geometry(
        jnp.arange(radial_total, dtype=jnp.int32), jnp.arange(polar_total, dtype=jnp.int32), radial_total, polar_total)
    padded = jnp.pad(test_fields, ((0, 0), (1, 1), (1, 1), (0, 0)))
    stepped = test_fields + diffuse(padded, outward, inward, metric, north_side, south_side) + source_step * sources(velocity, profiles)
    cos_table, sin_table = fourier_tables(0, NPHI)
    counts = jnp.broadcast_to(kept[None, :], (radial_total, polar_total)).reshape(-1)
    weights = mode_weights(counts)

    def filter_field(field_data):
        field_lines = field_data.reshape(-1, NPHI)
        cosine_part = jnp.dot(field_lines, cos_table.T, precision=lax.Precision.HIGHEST)
        sine_part = jnp.dot(field_lines, sin_table.T, precision=lax.Precision.HIGHEST)
        smooth = jnp.dot(cosine_part * weights, cos_table, precision=lax.Precision.HIGHEST)
        smooth = smooth + jnp.dot(sine_part * weights, sin_table, precision=lax.Precision.HIGHEST)
        return smooth.reshape(field_data.shape)

    filtered = lax.map(filter_field, stepped)
    result = jnp.where(polar_rows[None, None, :, None], filtered, stepped)
    emf = emf_terms(velocity, result) / NPHI
    return result, emf
```

```python
import functools
import math

import jax
import jax.numpy as jnp
import ml_dtypes
import numpy as np
from jax import lax
from jax.experimental import pallas as pl
from jax.experimental.pallas import tpu as pltpu
from jax.sharding import PartitionSpec as P

MESH = pl.DeviceIdType.MESH
NPHI = 2048
MMAX = 512
STAGES = 9
PHI = 8
F32 = jnp.float32
BF16 = jnp.bfloat16


def split_bf16(a):
    hi = a.astype(ml_dtypes.bfloat16)
    lo = (a - hi.astype(np.float64)).astype(ml_dtypes.bfloat16)
    return np.stack([hi, lo])


def fourier_constants():
    cell = np.arange(256)
    block = np.arange(64)

    def tables(mode):
        angle = 2.0 * math.pi * ((cell[:, None] * mode[None, :]) % NPHI) / NPHI
        return np.cos(angle), np.sin(angle)

    def scale(mode):
        return np.where(mode == 0, 1.0 / NPHI, 2.0 / NPHI)

    forward, inverse, modes = [], [], []
    singles, singles_back = [], []
    for r in (0, 4):
        mode = 8 * block + r
        c, s = tables(mode)
        full = np.concatenate([c, s], axis=1)
        singles.append(full)
        singles_back.append((full * np.tile(scale(mode), 2)).T)
        modes.append(np.tile(mode, 2))
    modes = [np.concatenate(modes)]
    for r in (1, 2, 3):
        m, n = 8 * block + r, 8 * block + 8 - r
        cm, sm = tables(m)
        cn, sn = tables(n)
        upper = np.concatenate([cm, sm, cn, sn], axis=1)
        lower = np.concatenate([-sm, cm, sn, -cn], axis=1)
        full = np.concatenate([upper, lower], axis=0)
        weights = np.concatenate([scale(m), scale(m), scale(n), scale(n)])
        forward.append(full)
        inverse.append((full * weights).T)
        modes.append(np.concatenate([m, m, n, n]))
    modes = np.broadcast_to(np.stack(modes).astype(np.float32)[:, None, :], (4, 8, 256))
    return (
        split_bf16(np.stack(forward)),
        split_bf16(np.stack(inverse)),
        split_bf16(np.stack(singles)),
        split_bf16(np.stack(singles_back)),
        np.ascontiguousarray(modes),
    )


def row_tables():
    j = np.arange(256)
    d = math.pi / 256
    angle = d * (j + 0.5)
    south = np.sin(angle + 0.5 * d) / np.sin(angle)
    north = np.sin(angle - 0.5 * d) / np.sin(angle)
    polar = (3 * (2 * j + 1) < 256) | (3 * (2 * (255 - j) + 1) < 256)
    kinds = np.stack([south, north, np.cos(angle), np.sin(angle), polar.astype(np.float64)])
    kinds = kinds.reshape(5, 8, 32).transpose(1, 0, 2)
    return np.ascontiguousarray(np.broadcast_to(kinds[..., None], (8, 5, 32, 128)).astype(np.float32))


def radial_constants():
    h = 0.3 / 8
    r = 0.7 + h * (np.arange(8) + 0.5)
    return ((r + h / 2) / r) ** 2, ((r - h / 2) / r) ** 2, (1.0 / r) ** 2


def split_rows(a):
    hi = a.astype(BF16).astype(F32)
    return jnp.concatenate([hi, a - hi], axis=0).astype(BF16)


def dot(a, b):
    return jnp.dot(a, b, preferred_element_type=F32)


def dot_split(a, high, low):
    lines = a.shape[0]
    both = split_rows(a)
    out = dot(both, high) + dot(both, low)
    return out[:lines] + out[lines:]


def filter_lines(blocks, keep, modes, fwd, inv, one, back):
    x0, x1, x2, x3, x4, x5, x6, x7 = blocks
    half = math.sqrt(0.5)
    s04, d04, s26, d26 = x0 + x4, x0 - x4, x2 + x6, x2 - x6
    s15, d15, s37, d37 = x1 + x5, x1 - x5, x3 + x7, x3 - x7
    even, odd = s04 + s26, s15 + s37
    cross, plus = half * (d15 - d37), half * (d15 + d37)
    pairs = [(d04 + cross, d26 + plus), (s04 - s26, s15 - s37), (d04 - cross, plus - d26)]

    def masked(mid, group):
        lines = mid.shape[0]
        kept = mid.reshape(lines // 8, 8, 256)
        kept = jnp.where((modes[group] < keep)[None], kept, 0.0)
        return kept.reshape(lines, 256)

    mid = jnp.concatenate(
        [dot_split(even + odd, one[0, 0], one[1, 0]), dot_split(even - odd, one[0, 1], one[1, 1])], axis=1
    )
    mid = masked(mid, 0)
    p0 = dot_split(mid[:, :128], back[0, 0], back[1, 0])
    p4 = dot_split(mid[:, 128:], back[0, 1], back[1, 1])
    p, q = [], []
    for r, (u, v) in enumerate(pairs):
        mid = dot_split(jnp.concatenate([u, v], axis=1), fwd[0, r], fwd[1, r])
        mid = masked(mid, r + 1)
        out = dot_split(mid, inv[0, r], inv[1, r])
        p.append(out[:, :256])
        q.append(out[:, 256:])
    (p1, p2, p3), (q1, q2, q3) = p, q
    a, b = p0 + p4, p0 - p4
    p13, q13 = p1 + p3, q1 - q3
    ph, qh = half * (p1 - p3), half * (q1 + q3)
    ap, am, bp, bm = a + p2, a - p2, b + q2, b - q2
    return [
        ap + p13,
        bp + (ph + qh),
        am + q13,
        bm - (ph - qh),
        ap - p13,
        bp - (ph + qh),
        am - q13,
        bm + (ph - qh),
    ]


def kernel(
    tf, vel, kept, tab_hbm, fwd_hbm, inv_hbm, one_hbm, back_hbm, modes_hbm,
    out, emf,
    xp, v, tab, fwd, inv, one, back, modes,
    edge, halo_t, halo_r, coef, keep, st, rx, yb, res, acc, got,
    load_sem, theta_send, theta_recv, row_send, row_recv, keep_send, keep_recv,
    a_send, a_recv, b_send, b_recv, out_sem, emf_send, emf_recv,
):
    phi, theta, row = lax.axis_index("phi"), lax.axis_index("theta"), lax.axis_index("row")
    heavy = (theta == 0) | (theta == 7)
    light = (theta == 1) | (theta == 6)
    helper = (theta == 2) | (theta == 5)
    source = heavy | light
    worker = source | helper
    partner = jnp.where(theta == 0, 2, jnp.where(theta == 2, 0, jnp.where(theta == 7, 5, 7)))
    octet = jnp.where(helper | (theta == 6), 2, 0)
    my_i, my_o = phi // 2, octet + phi % 2

    def others(k):
        return lax.rem(phi + k, PHI)

    loads = [
        pltpu.make_async_copy(tf, xp.at[:, :, pl.ds(8, 32), :], load_sem.at[0]),
        pltpu.make_async_copy(vel, v, load_sem.at[1]),
        pltpu.make_async_copy(tab_hbm.at[theta], tab, load_sem.at[2]),
        pltpu.make_async_copy(fwd_hbm, fwd, load_sem.at[3]),
        pltpu.make_async_copy(inv_hbm, inv, load_sem.at[4]),
        pltpu.make_async_copy(one_hbm, one, load_sem.at[5]),
        pltpu.make_async_copy(back_hbm, back, load_sem.at[6]),
        pltpu.make_async_copy(modes_hbm, modes, load_sem.at[7]),
    ]
    for load in loads:
        load.start()

    barrier = pltpu.get_barrier_semaphore()
    pl.semaphore_signal(barrier, inc=1, device_id={"row": 1 - row}, device_id_type=MESH)
    for k in range(1, PHI):
        pl.semaphore_signal(barrier, inc=1, device_id={"phi": others(k)}, device_id_type=MESH)

    @pl.when(theta > 0)
    def _():
        pl.semaphore_signal(barrier, inc=1, device_id={"theta": theta - 1}, device_id_type=MESH)

    @pl.when(theta < 7)
    def _():
        pl.semaphore_signal(barrier, inc=1, device_id={"theta": theta + 1}, device_id_type=MESH)

    @pl.when(heavy | helper)
    def _():
        for k in range(PHI):
            pl.semaphore_signal(
                barrier, inc=1, device_id={"theta": partner, "phi": others(k)}, device_id_type=MESH
            )

    loads[0].wait()

    def pack(f, _):
        for i in range(4):
            edge[0, f, pl.ds(i, 1), :] = xp[f, i, pl.ds(8, 1), :]
            edge[1, f, pl.ds(i, 1), :] = xp[f, i, pl.ds(39, 1), :]
        return 0

    lax.fori_loop(0, 27, pack, 0)
    eye = lax.broadcasted_iota(jnp.int32, (32, 32), 0) == lax.broadcasted_iota(jnp.int32, (32, 32), 1)
    counts = jnp.where(eye, jnp.broadcast_to(kept[...], (32, 32)), 0).astype(F32)
    keep[0] = jnp.broadcast_to(jnp.sum(counts, axis=1, keepdims=True), (32, 128))

    peers = PHI + jnp.where(theta > 0, 1, 0) + jnp.where(theta < 7, 1, 0) + jnp.where(heavy | helper, PHI, 0)
    pl.semaphore_wait(barrier, peers)

    def theta_copy(side, there):
        return pltpu.make_async_remote_copy(
            src_ref=edge.at[side], dst_ref=halo_t.at[side], send_sem=theta_send.at[side],
            recv_sem=theta_recv.at[side], device_id={"theta": there}, device_id_type=MESH)

    @pl.when(theta > 0)
    def _():
        theta_copy(0, theta - 1).start()

    @pl.when(theta < 7)
    def _():
        theta_copy(1, theta + 1).start()

    keep_copy = pltpu.make_async_remote_copy(
        src_ref=keep.at[0], dst_ref=keep.at[1], send_sem=keep_send, recv_sem=keep_recv,
        device_id={"theta": partner}, device_id_type=MESH)

    @pl.when(heavy)
    def _():
        keep_copy.start()

    edge_i = jnp.where(row == 0, 3, 0)

    def row_copy(n):
        return pltpu.make_async_remote_copy(
            src_ref=xp.at[pl.ds(3 * n, 3), edge_i, pl.ds(8, 32), :], dst_ref=halo_r.at[pl.ds(3 * n, 3)],
            send_sem=row_send, recv_sem=row_recv.at[n],
            device_id={"row": 1 - row}, device_id_type=MESH)

    def send_row(n, _):
        row_copy(n).start()
        return 0

    lax.fori_loop(0, STAGES, send_row, 0)

    for load in loads[1:]:
        load.wait()
    outward, inward, metric = radial_constants()

    def radial(values, i):
        return jnp.where(row == 0, F32(values[i]), F32(values[i + 4]))

    south, north = tab[0], tab[1]
    for i in range(4):
        g = 0.1 * radial(metric, i)
        cs, cn = g * south, g * north
        both = 0.2 * (radial(outward, i) + radial(inward, i))
        centre = (1.0 - both) - (cs + cn)
        for lanes in range(2):
            part = pl.ds(128 * lanes, 128)
            coef[0, i, :, part] = cs
            coef[1, i, :, part] = cn
            coef[2, i, :, part] = centre

    @pl.when(theta < 7)
    def _():
        theta_copy(0, theta).wait_recv()

    @pl.when(theta > 0)
    def _():
        theta_copy(1, theta).wait_recv()

    @pl.when(theta == 7)
    def _():
        halo_t[0] = jnp.zeros((27, 4, 256), F32)

    @pl.when(theta == 0)
    def _():
        halo_t[1] = jnp.zeros((27, 4, 256), F32)

    inner = jnp.where(row == 1, F32(1.0), F32(0.0))
    outer = jnp.where(row == 0, F32(1.0), F32(0.0))

    def a_copy(n, k, there, o_base, sem):
        p = others(k)
        i, o = p // 2, o_base + p % 2
        return pltpu.make_async_remote_copy(
            src_ref=st.at[pl.ds(3 * n, 3), i, pl.ds(pl.multiple_of(o * 8, 8), 8), :],
            dst_ref=rx.at[n, phi], send_sem=a_send.at[sem], recv_sem=a_recv.at[n],
            device_id={"theta": there, "phi": p}, device_id_type=MESH)

    def step(n, _):
        p_unit, q_unit = n // 3, n % 3
        row_copy(n).wait_recv()
        unit = [jnp.where(p_unit == k, F32(0.5), F32(0.0)) for k in range(3)]
        weight = [jnp.where(q_unit == k, F32(1.0), F32(0.0)) for k in range(3)]
        profile = weight[0] + weight[1] * tab[2] + weight[2] * tab[3]
        profile = jnp.concatenate([profile, profile], axis=1)
        for c in range(3):
            f = 3 * n + c
            for i in range(4):
                xp[f, i, pl.ds(7, 1), :] = halo_t[1, f, pl.ds(i, 1), :]
                xp[f, i, pl.ds(40, 1), :] = halo_t[0, f, pl.ds(i, 1), :]
        for i in range(4):
            v0, v1, v2 = v[0, i], v[1, i], v[2, i]
            turned = (v1 * unit[2] - v2 * unit[1], v2 * unit[0] - v0 * unit[2], v0 * unit[1] - v1 * unit[0])
            for c in range(3):
                f = 3 * n + c
                b = xp[f, i, pl.ds(8, 32), :]
                up = xp[f, i + 1, pl.ds(8, 32), :] if i < 3 else halo_r[f]
                down = xp[f, i - 1, pl.ds(8, 32), :] if i > 0 else halo_r[f]
                cu, cd = 0.2 * radial(outward, i), 0.2 * radial(inward, i)
                if i == 3:
                    cu = cu * outer
                if i == 0:
                    cd = cd * inner
                total = coef[2, i] * b + cu * up + cd * down + profile * turned[c]
                total = total + coef[0, i] * xp[f, i, pl.ds(9, 32), :] + coef[1, i] * xp[f, i, pl.ds(7, 32), :]
                st[f, i] = total

        @pl.when(source)
        def _():
            pltpu.make_async_copy(
                st.at[pl.ds(3 * n, 3), my_i, pl.ds(pl.multiple_of(my_o * 8, 8), 8), :], rx.at[n, phi], a_recv.at[n]
            ).start()
            for k in range(1, PHI):
                a_copy(n, k, theta, octet, 0).start()

        @pl.when(heavy)
        def _():
            for k in range(PHI):
                a_copy(n, k, partner, 2, 1).start()

        @pl.when(light)
        def _():
            rest = pl.ds(pl.multiple_of(16 - 8 * octet, 8), 16)
            for c in range(3):
                res[3 * n + c, :, rest, :] = st[3 * n + c, :, rest, :]

        @pl.when(jnp.logical_not(source))
        def _():
            for c in range(3):
                res[3 * n + c] = st[3 * n + c]

        return 0

    lax.fori_loop(0, STAGES, step, 0)

    home = jnp.where(helper, partner, theta)

    def b_copy(n, p):
        return pltpu.make_async_remote_copy(
            src_ref=yb.at[n, p],
            dst_ref=res.at[pl.ds(3 * n, 3), my_i, pl.ds(pl.multiple_of(my_o * 8, 8), 8), :],
            send_sem=b_send, recv_sem=b_recv.at[n],
            device_id={"theta": home, "phi": p}, device_id_type=MESH)

    @pl.when(worker)
    def _():
        @pl.when(helper)
        def _():
            keep_copy.wait_recv()

        mine = pl.ds(pl.multiple_of(my_o * 8, 8), 8)
        which = jnp.where(helper, 1, 0)
        kept_rows = keep[which, mine, :]
        kept_rows = jnp.concatenate([kept_rows, kept_rows], axis=1)
        polar = jnp.maximum(tab[4, mine, :], jnp.where(helper, F32(1.0), F32(0.0)))
        polar = jnp.concatenate([polar, polar], axis=1) > 0.5

        def work(n, _):
            pltpu.make_async_copy(rx.at[n], rx.at[n], a_recv.at[n]).wait()
            blocks = [rx[n, p].reshape(24, 256) for p in range(PHI)]
            done = filter_lines(blocks, kept_rows, modes, fwd, inv, one, back)
            for p in range(PHI):
                yb[n, p] = jnp.where(polar[None], done[p].reshape(3, 8, 256), rx[n, p])

            for k in range(1, PHI):
                b_copy(n, others(k)).start()

            @pl.when(helper)
            def _():
                b_copy(n, phi).start()

            @pl.when(source)
            def _():
                pltpu.make_async_copy(
                    yb.at[n, phi],
                    res.at[pl.ds(3 * n, 3), my_i, pl.ds(pl.multiple_of(my_o * 8, 8), 8), :],
                    b_recv.at[n],
                ).start()

            return 0

        lax.fori_loop(0, STAGES, work, 0)

    acc[...] = jnp.zeros((32, 128), F32)
    lane = lax.broadcasted_iota(jnp.int32, (32, 128), 1)

    def out_copy(n):
        return pltpu.make_async_copy(res.at[pl.ds(3 * n, 3)], out.at[pl.ds(3 * n, 3)], out_sem.at[n])

    def finish(n, _):
        @pl.when(heavy)
        def _():
            whole = res.at[pl.ds(3 * n, 3)]
            pltpu.make_async_copy(whole, whole, b_recv.at[n]).wait()

        @pl.when(light)
        def _():
            part = res.at[pl.ds(3 * n, 3), :, pl.ds(pl.multiple_of(octet * 8, 8), 16), :]
            pltpu.make_async_copy(part, part, b_recv.at[n]).wait()

        out_copy(n).start()
        total = acc[...]
        for i in range(4):
            v0, v1, v2 = v[0, i], v[1, i], v[2, i]
            r0, r1, r2 = res[3 * n, i], res[3 * n + 1, i], res[3 * n + 2, i]
            terms = (v1 * r2 - v2 * r1, v2 * r0 - v0 * r2, v0 * r1 - v1 * r0)
            for c in range(3):
                summed = jnp.sum(terms[c][:, :128] + terms[c][:, 128:], axis=1, keepdims=True)
                total = jnp.where(lane == 4 * (3 * n + c) + i, jnp.broadcast_to(summed, (32, 128)), total)
        acc[...] = total
        return 0

    lax.fori_loop(0, STAGES, finish, 0)

    def emf_copy(k):
        p = others(k)
        return pltpu.make_async_remote_copy(
            src_ref=acc.at[pl.ds(pl.multiple_of(p // 2 * 8, 8), 8), :], dst_ref=got.at[phi],
            send_sem=emf_send, recv_sem=emf_recv, device_id={"phi": p}, device_id_type=MESH)

    for k in range(1, PHI):
        emf_copy(k).start()
    pltpu.make_async_copy(acc.at[pl.ds(pl.multiple_of(phi // 2 * 8, 8), 8), :], got.at[phi], emf_recv).start()
    pltpu.make_async_copy(got, got, emf_recv).wait()
    summed = got[0]
    for p in range(1, PHI):
        summed = summed + got[p]
    summed = summed * (1.0 / NPHI)
    emf[...] = jnp.where(phi % 2 == 0, summed[:4], summed[4:])

    def drain(ref, sem):
        pltpu.make_async_copy(ref, ref, sem).wait()

    seven = got.at[pl.ds(0, 7)]
    drain(seven, emf_send)
    drain(halo_r, row_send)

    @pl.when(theta > 0)
    def _():
        theta_copy(0, theta).wait_send()

    @pl.when(theta < 7)
    def _():
        theta_copy(1, theta).wait_send()

    @pl.when(heavy)
    def _():
        keep_copy.wait_send()
        drain(rx, a_send.at[1])

    @pl.when(source)
    def _():
        drain(rx.at[:, pl.ds(0, 7)], a_send.at[0])
        drain(yb.at[:, pl.ds(0, 7)], b_send)

    @pl.when(helper)
    def _():
        drain(yb, b_send)

    def drain_out(n, _):
        out_copy(n).wait()
        return 0

    lax.fori_loop(0, STAGES, drain_out, 0)


def body(test_fields, velocity, kept):
    forward, inverse, singles, singles_back, modes = fourier_constants()
    tables = row_tables()
    hbm, vmem = pl.BlockSpec(memory_space=pl.ANY), pl.BlockSpec(memory_space=pltpu.VMEM)
    dma, regular = pltpu.SemaphoreType.DMA, pltpu.SemaphoreType.REGULAR
    del regular
    result, emf = pl.pallas_call(
        kernel,
        out_shape=(
            jax.ShapeDtypeStruct((27, 4, 32, 256), F32),
            jax.ShapeDtypeStruct((4, 128), F32),
        ),
        in_specs=[hbm, hbm, vmem] + [hbm] * 6,
        out_specs=(hbm, vmem),
        scratch_shapes=[
            pltpu.VMEM((27, 4, 48, 256), F32),
            pltpu.VMEM((3, 4, 32, 256), F32),
            pltpu.VMEM((5, 32, 128), F32),
            pltpu.VMEM(forward.shape, BF16),
            pltpu.VMEM(inverse.shape, BF16),
            pltpu.VMEM(singles.shape, BF16),
            pltpu.VMEM(singles_back.shape, BF16),
            pltpu.VMEM(modes.shape, F32),
            pltpu.VMEM((2, 27, 4, 256), F32),
            pltpu.VMEM((2, 27, 4, 256), F32),
            pltpu.VMEM((27, 32, 256), F32),
            pltpu.VMEM((3, 4, 32, 256), F32),
            pltpu.VMEM((2, 32, 128), F32),
            pltpu.VMEM((27, 4, 32, 256), F32),
            pltpu.VMEM((STAGES, PHI, 3, 8, 256), F32),
            pltpu.VMEM((STAGES, PHI, 3, 8, 256), F32),
            pltpu.VMEM((27, 4, 32, 256), F32),
            pltpu.VMEM((32, 128), F32),
            pltpu.VMEM((PHI, 8, 128), F32),
            dma((8,)),
            dma((2,)),
            dma((2,)),
            dma,
            dma((STAGES,)),
            dma,
            dma,
            dma((2,)),
            dma((STAGES,)),
            dma,
            dma((STAGES,)),
            dma((STAGES,)),
            dma,
            dma,
        ],
        compiler_params=pltpu.CompilerParams(
            collective_id=0, has_side_effects=True, vmem_limit_bytes=48 * 2**20
        ),
        name="substep",
    )(
        test_fields, velocity, kept.reshape(1, 32), jnp.asarray(tables), jnp.asarray(forward),
        jnp.asarray(inverse), jnp.asarray(singles), jnp.asarray(singles_back), jnp.asarray(modes),
    )
    emf = emf[:, :108].T.reshape(27, 4, 4)
    return result, emf


def solution(mesh):
    return jax.shard_map(
        body,
        mesh=mesh,
        in_specs=(P(None, "row", "theta", "phi"), P(None, "row", "theta", "phi"), P("theta")),
        out_specs=(P(None, "row", "theta", "phi"), P(None, "row", ("theta", "phi"))),
        check_vma=False,
    )
```

```python
import functools
import math

import jax
import jax.numpy as jnp
import ml_dtypes
import numpy as np
from jax import lax
from jax.experimental import pallas as pl
from jax.experimental.pallas import tpu as pltpu
from jax.sharding import PartitionSpec as P

MESH = pl.DeviceIdType.MESH
NPHI = 2048
MMAX = 512
STAGES = 9
AHEAD = 2
ACROSS = 2
LAG = 4
BEHIND = 1
HELP = 0
PHI = 8
F32 = jnp.float32
BF16 = jnp.bfloat16


def split_bf16(a):
    hi = a.astype(ml_dtypes.bfloat16)
    lo = (a - hi.astype(np.float64)).astype(ml_dtypes.bfloat16)
    return np.stack([hi, lo])


def fourier_constants():
    cell = np.arange(256)
    block = np.arange(64)

    def tables(mode):
        angle = 2.0 * math.pi * ((cell[:, None] * mode[None, :]) % NPHI) / NPHI
        return np.cos(angle), np.sin(angle)

    def scale(mode):
        return np.where(mode == 0, 1.0 / NPHI, 2.0 / NPHI)

    forward, inverse, modes = [], [], []
    singles, singles_back = [], []
    for r in (0, 4):
        mode = 8 * block + r
        c, s = tables(mode)
        full = np.concatenate([c, s], axis=1)
        singles.append(full)
        singles_back.append((full * np.tile(scale(mode), 2)).T)
        modes.append(np.tile(mode, 2))
    modes = [np.concatenate(modes)]
    for r in (1, 2, 3):
        m, n = 8 * block + r, 8 * block + 8 - r
        cm, sm = tables(m)
        cn, sn = tables(n)
        upper = np.concatenate([cm, sm, cn, sn], axis=1)
        lower = np.concatenate([-sm, cm, sn, -cn], axis=1)
        full = np.concatenate([upper, lower], axis=0)
        weights = np.concatenate([scale(m), scale(m), scale(n), scale(n)])
        forward.append(full)
        inverse.append((full * weights).T)
        modes.append(np.concatenate([m, m, n, n]))
    modes = np.broadcast_to(np.stack(modes).astype(np.float32)[:, None, :], (4, 8, 256))
    return (
        split_bf16(np.stack(forward)),
        split_bf16(np.stack(inverse)),
        split_bf16(np.stack(singles)),
        split_bf16(np.stack(singles_back)),
        np.ascontiguousarray(modes),
    )


def row_tables():
    j = np.arange(256)
    d = math.pi / 256
    angle = d * (j + 0.5)
    south = np.sin(angle + 0.5 * d) / np.sin(angle)
    north = np.sin(angle - 0.5 * d) / np.sin(angle)
    polar = (3 * (2 * j + 1) < 256) | (3 * (2 * (255 - j) + 1) < 256)
    kinds = np.stack([south, north, np.cos(angle), np.sin(angle), polar.astype(np.float64)])
    kinds = kinds.reshape(5, 8, 32).transpose(1, 0, 2)
    return np.ascontiguousarray(np.broadcast_to(kinds[..., None], (8, 5, 32, 128)).astype(np.float32))


def radial_constants():
    h = 0.3 / 8
    r = 0.7 + h * (np.arange(8) + 0.5)
    return ((r + h / 2) / r) ** 2, ((r - h / 2) / r) ** 2, (1.0 / r) ** 2


def split_rows(a):
    hi = a.astype(BF16).astype(F32)
    return jnp.concatenate([hi, a - hi], axis=0).astype(BF16)


def dot(a, b):
    return jnp.dot(a, b, preferred_element_type=F32)


def dot_split(a, high, low):
    lines = a.shape[0]
    both = split_rows(a)
    out = dot(both, high) + dot(both, low)
    return out[:lines] + out[lines:]


def filter_lines(blocks, keep, modes, fwd, inv, one, back):
    x0, x1, x2, x3, x4, x5, x6, x7 = blocks
    half = math.sqrt(0.5)
    s04, d04, s26, d26 = x0 + x4, x0 - x4, x2 + x6, x2 - x6
    s15, d15, s37, d37 = x1 + x5, x1 - x5, x3 + x7, x3 - x7
    even, odd = s04 + s26, s15 + s37
    cross, plus = half * (d15 - d37), half * (d15 + d37)
    pairs = [(d04 + cross, d26 + plus), (s04 - s26, s15 - s37), (d04 - cross, plus - d26)]

    def masked(mid, group):
        lines = mid.shape[0]
        kept = mid.reshape(lines // 8, 8, 256)
        kept = jnp.where((modes[group] < keep)[None], kept, 0.0)
        return kept.reshape(lines, 256)

    mid = jnp.concatenate(
        [dot_split(even + odd, one[0, 0], one[1, 0]), dot_split(even - odd, one[0, 1], one[1, 1])], axis=1
    )
    mid = masked(mid, 0)
    p0 = dot_split(mid[:, :128], back[0, 0], back[1, 0])
    p4 = dot_split(mid[:, 128:], back[0, 1], back[1, 1])
    p, q = [], []
    for r, (u, v) in enumerate(pairs):
        mid = dot_split(jnp.concatenate([u, v], axis=1), fwd[0, r], fwd[1, r])
        mid = masked(mid, r + 1)
        out = dot_split(mid, inv[0, r], inv[1, r])
        p.append(out[:, :256])
        q.append(out[:, 256:])
    (p1, p2, p3), (q1, q2, q3) = p, q
    a, b = p0 + p4, p0 - p4
    p13, q13 = p1 + p3, q1 - q3
    ph, qh = half * (p1 - p3), half * (q1 + q3)
    ap, am, bp, bm = a + p2, a - p2, b + q2, b - q2
    return [
        ap + p13,
        bp + (ph + qh),
        am + q13,
        bm - (ph - qh),
        ap - p13,
        bp - (ph + qh),
        am - q13,
        bm + (ph - qh),
    ]


def kernel(
    tf, vel, kept, tab_hbm, fwd_hbm, inv_hbm, one_hbm, back_hbm, modes_hbm,
    out, emf,
    xp, v, tab, fwd, inv, one, back, modes,
    edge, halo_t, halo_r, coef, keep, st, rx, yb, res, rel, acc, got,
    load_sem, theta_send, theta_recv, row_send, row_recv, keep_send, keep_recv,
    a_send, across_send, a_recv, b_send, b_recv, rel_send, rel_recv, out_sem, emf_send, emf_recv,
):
    phi, theta, row = lax.axis_index("phi"), lax.axis_index("theta"), lax.axis_index("row")
    heavy = (theta == 0) | (theta == 7)
    light = (theta == 1) | (theta == 6)
    helper = (theta == 2) | (theta == 5)
    source = heavy | light
    worker = source | helper
    partner = jnp.where(theta == 0, 2, jnp.where(theta == 2, 0, jnp.where(theta == 7, 5, 7)))
    octet = jnp.where(helper | (theta == 6), 2, 0)
    my_i, my_o = phi // 2, octet + phi % 2

    def others(k):
        return lax.rem(phi + k, PHI)

    loads = [
        pltpu.make_async_copy(tf, xp.at[:, :, pl.ds(8, 32), :], load_sem.at[0]),
        pltpu.make_async_copy(vel, v, load_sem.at[1]),
        pltpu.make_async_copy(tab_hbm.at[theta], tab, load_sem.at[2]),
        pltpu.make_async_copy(fwd_hbm, fwd, load_sem.at[3]),
        pltpu.make_async_copy(inv_hbm, inv, load_sem.at[4]),
        pltpu.make_async_copy(one_hbm, one, load_sem.at[5]),
        pltpu.make_async_copy(back_hbm, back, load_sem.at[6]),
        pltpu.make_async_copy(modes_hbm, modes, load_sem.at[7]),
    ]
    for load in loads:
        load.start()

    barrier = pltpu.get_barrier_semaphore()
    pl.semaphore_signal(barrier, inc=1, device_id={"row": 1 - row}, device_id_type=MESH)
    for k in range(1, PHI):
        pl.semaphore_signal(barrier, inc=1, device_id={"phi": others(k)}, device_id_type=MESH)

    @pl.when(theta > 0)
    def _():
        pl.semaphore_signal(barrier, inc=1, device_id={"theta": theta - 1}, device_id_type=MESH)

    @pl.when(theta < 7)
    def _():
        pl.semaphore_signal(barrier, inc=1, device_id={"theta": theta + 1}, device_id_type=MESH)

    @pl.when(heavy | helper)
    def _():
        for k in range(PHI):
            pl.semaphore_signal(
                barrier, inc=1, device_id={"theta": partner, "phi": others(k)}, device_id_type=MESH
            )

    loads[0].wait()

    def pack(f, _):
        for i in range(4):
            edge[0, f, pl.ds(i, 1), :] = xp[f, i, pl.ds(8, 1), :]
            edge[1, f, pl.ds(i, 1), :] = xp[f, i, pl.ds(39, 1), :]
        return 0

    lax.fori_loop(0, 27, pack, 0)
    eye = lax.broadcasted_iota(jnp.int32, (32, 32), 0) == lax.broadcasted_iota(jnp.int32, (32, 32), 1)
    counts = jnp.where(eye, jnp.broadcast_to(kept[...], (32, 32)), 0).astype(F32)
    keep[0] = jnp.broadcast_to(jnp.sum(counts, axis=1, keepdims=True), (32, 128))

    peers = PHI + jnp.where(theta > 0, 1, 0) + jnp.where(theta < 7, 1, 0) + jnp.where(heavy | helper, PHI, 0)
    pl.semaphore_wait(barrier, peers)

    def theta_copy(side, there):
        return pltpu.make_async_remote_copy(
            src_ref=edge.at[side], dst_ref=halo_t.at[side], send_sem=theta_send.at[side],
            recv_sem=theta_recv.at[side], device_id={"theta": there}, device_id_type=MESH)

    @pl.when(theta > 0)
    def _():
        theta_copy(0, theta - 1).start()

    @pl.when(theta < 7)
    def _():
        theta_copy(1, theta + 1).start()

    keep_copy = pltpu.make_async_remote_copy(
        src_ref=keep.at[0], dst_ref=keep.at[1], send_sem=keep_send, recv_sem=keep_recv,
        device_id={"theta": partner}, device_id_type=MESH)

    @pl.when(heavy)
    def _():
        keep_copy.start()

    edge_i = jnp.where(row == 0, 3, 0)

    def row_copy(n):
        return pltpu.make_async_remote_copy(
            src_ref=xp.at[pl.ds(3 * n, 3), edge_i, pl.ds(8, 32), :], dst_ref=halo_r.at[pl.ds(3 * n, 3)],
            send_sem=row_send.at[n], recv_sem=row_recv.at[n],
            device_id={"row": 1 - row}, device_id_type=MESH)

    for n in range(AHEAD):
        row_copy(n).start()

    for load in loads[1:]:
        load.wait()
    outward, inward, metric = radial_constants()

    def radial(values, i):
        return jnp.where(row == 0, F32(values[i]), F32(values[i + 4]))

    south, north = tab[0], tab[1]
    for i in range(4):
        g = 0.1 * radial(metric, i)
        cs, cn = g * south, g * north
        both = 0.2 * (radial(outward, i) + radial(inward, i))
        centre = (1.0 - both) - (cs + cn)
        for lanes in range(2):
            part = pl.ds(128 * lanes, 128)
            coef[0, i, :, part] = cs
            coef[1, i, :, part] = cn
            coef[2, i, :, part] = centre

    @pl.when(theta < 7)
    def _():
        theta_copy(0, theta).wait_recv()

    @pl.when(theta > 0)
    def _():
        theta_copy(1, theta).wait_recv()

    @pl.when(theta == 7)
    def _():
        halo_t[0] = jnp.zeros((27, 4, 256), F32)

    @pl.when(theta == 0)
    def _():
        halo_t[1] = jnp.zeros((27, 4, 256), F32)

    inner = jnp.where(row == 1, F32(1.0), F32(0.0))
    outer = jnp.where(row == 0, F32(1.0), F32(0.0))

    def drain(ref, sem):
        pltpu.make_async_copy(ref, ref, sem).wait()

    def a_copy(n, k, there, o_base, sem):
        p = others(k)
        i, o = p // 2, o_base + p % 2
        return pltpu.make_async_remote_copy(
            src_ref=st.at[pl.ds(3 * n, 3), i, pl.ds(pl.multiple_of(o * 8, 8), 8), :],
            dst_ref=rx.at[n, phi], send_sem=sem, recv_sem=a_recv.at[n],
            device_id={"theta": there, "phi": p}, device_id_type=MESH)

    def across_copy(n, k):
        return a_copy(n, k, partner, 2, across_send.at[lax.rem(n, ACROSS)])

    def step(n):
        p_unit, q_unit = n // 3, n % 3
        row_copy(n).wait_recv()
        row_copy(n).wait_send()

        @pl.when(n + AHEAD < STAGES)
        def _():
            row_copy(n + AHEAD).start()

        unit = [jnp.where(p_unit == k, F32(0.5), F32(0.0)) for k in range(3)]
        weight = [jnp.where(q_unit == k, F32(1.0), F32(0.0)) for k in range(3)]
        profile = weight[0] + weight[1] * tab[2] + weight[2] * tab[3]
        profile = jnp.concatenate([profile, profile], axis=1)
        for c in range(3):
            f = 3 * n + c
            for i in range(4):
                xp[f, i, pl.ds(7, 1), :] = halo_t[1, f, pl.ds(i, 1), :]
                xp[f, i, pl.ds(40, 1), :] = halo_t[0, f, pl.ds(i, 1), :]
        for i in range(4):
            v0, v1, v2 = v[0, i], v[1, i], v[2, i]
            turned = (v1 * unit[2] - v2 * unit[1], v2 * unit[0] - v0 * unit[2], v0 * unit[1] - v1 * unit[0])
            for c in range(3):
                f = 3 * n + c
                b = xp[f, i, pl.ds(8, 32), :]
                up = xp[f, i + 1, pl.ds(8, 32), :] if i < 3 else halo_r[f]
                down = xp[f, i - 1, pl.ds(8, 32), :] if i > 0 else halo_r[f]
                cu, cd = 0.2 * radial(outward, i), 0.2 * radial(inward, i)
                if i == 3:
                    cu = cu * outer
                if i == 0:
                    cd = cd * inner
                total = coef[2, i] * b + cu * up + cd * down + profile * turned[c]
                total = total + coef[0, i] * xp[f, i, pl.ds(9, 32), :] + coef[1, i] * xp[f, i, pl.ds(7, 32), :]
                st[f, i] = total

        @pl.when(source)
        def _():
            pltpu.make_async_copy(
                st.at[pl.ds(3 * n, 3), my_i, pl.ds(pl.multiple_of(my_o * 8, 8), 8), :], rx.at[n, phi], a_recv.at[n]
            ).start()
            for k in range(1, PHI):
                a_copy(n, k, theta, octet, a_send).start()

        @pl.when(heavy)
        def _():
            @pl.when(n >= ACROSS)
            def _():
                drain(rx.at[0], across_send.at[lax.rem(n, ACROSS)])

            for k in range(PHI):
                across_copy(n, k).start()

        @pl.when(light)
        def _():
            rest = pl.ds(pl.multiple_of(16 - 8 * octet, 8), 16)
            for c in range(3):
                res[3 * n + c, :, rest, :] = st[3 * n + c, :, rest, :]

        @pl.when(jnp.logical_not(source))
        def _():
            for c in range(3):
                res[3 * n + c] = st[3 * n + c]

    def b_copy(n, p):
        return pltpu.make_async_remote_copy(
            src_ref=yb.at[n, p],
            dst_ref=res.at[pl.ds(3 * n, 3), my_i, pl.ds(pl.multiple_of(my_o * 8, 8), 8), :],
            send_sem=b_send, recv_sem=b_recv.at[n],
            device_id={"phi": p}, device_id_type=MESH)

    relay_rows = pl.ds(pl.multiple_of(phi % 2 * 8, 8), 8)

    def gather_copy(n, p):
        return pltpu.make_async_remote_copy(
            src_ref=yb.at[n, p], dst_ref=rel.at[n, :, my_i, relay_rows, :],
            send_sem=b_send, recv_sem=rel_recv.at[n], device_id={"phi": p}, device_id_type=MESH)

    def relay(n):
        pltpu.make_async_copy(rel.at[n], rel.at[n], rel_recv.at[n]).wait()
        pltpu.make_async_remote_copy(
            src_ref=rel.at[n], dst_ref=res.at[pl.ds(3 * n, 3), :, pl.ds(16, 16), :],
            send_sem=rel_send, recv_sem=b_recv.at[n], device_id={"theta": partner}, device_id_type=MESH,
        ).start()

    mine = pl.ds(pl.multiple_of(my_o * 8, 8), 8)

    def work(n):
        @pl.when(helper & (n == 0))
        def _():
            keep_copy.wait_recv()

        kept_rows = keep[jnp.where(helper, 1, 0), mine, :]
        kept_rows = jnp.concatenate([kept_rows, kept_rows], axis=1)
        polar = jnp.maximum(tab[4, mine, :], jnp.where(helper, F32(1.0), F32(0.0)))
        polar = jnp.concatenate([polar, polar], axis=1) > 0.5
        pltpu.make_async_copy(rx.at[n], rx.at[n], a_recv.at[n]).wait()
        blocks = [rx[n, p].reshape(24, 256) for p in range(PHI)]
        done = filter_lines(blocks, kept_rows, modes, fwd, inv, one, back)
        for p in range(PHI):
            yb[n, p] = jnp.where(polar[None], done[p].reshape(3, 8, 256), rx[n, p])

        @pl.when(source)
        def _():
            pltpu.make_async_copy(
                yb.at[n, phi],
                res.at[pl.ds(3 * n, 3), my_i, pl.ds(pl.multiple_of(my_o * 8, 8), 8), :],
                b_recv.at[n],
            ).start()
            for k in range(1, PHI):
                b_copy(n, others(k)).start()

        @pl.when(helper)
        def _():
            pltpu.make_async_copy(yb.at[n, phi], rel.at[n, :, my_i, relay_rows, :], rel_recv.at[n]).start()
            for k in range(1, PHI):
                gather_copy(n, others(k)).start()

    acc[...] = jnp.zeros((32, 128), F32)
    lane = lax.broadcasted_iota(jnp.int32, (32, 128), 1)

    def out_copy(n):
        return pltpu.make_async_copy(res.at[pl.ds(3 * n, 3)], out.at[pl.ds(3 * n, 3)], out_sem.at[n])

    def finish(n):
        @pl.when(heavy)
        def _():
            whole = res.at[pl.ds(3 * n, 3)]
            pltpu.make_async_copy(whole, whole, b_recv.at[n]).wait()

        @pl.when(light)
        def _():
            part = res.at[pl.ds(3 * n, 3), :, pl.ds(pl.multiple_of(octet * 8, 8), 16), :]
            pltpu.make_async_copy(part, part, b_recv.at[n]).wait()

        out_copy(n).start()
        total = acc[...]
        for i in range(4):
            v0, v1, v2 = v[0, i], v[1, i], v[2, i]
            r0, r1, r2 = res[3 * n, i], res[3 * n + 1, i], res[3 * n + 2, i]
            terms = (v1 * r2 - v2 * r1, v2 * r0 - v0 * r2, v0 * r1 - v1 * r0)
            for c in range(3):
                summed = jnp.sum(terms[c][:, :128] + terms[c][:, 128:], axis=1, keepdims=True)
                total = jnp.where(lane == 4 * (3 * n + c) + i, jnp.broadcast_to(summed, (32, 128)), total)
        acc[...] = total

    def tick(t, _):
        @pl.when(t < STAGES)
        def _():
            step(t)

        now = jnp.where(helper, t - HELP, t - BEHIND)

        @pl.when(worker & (now >= 0) & (now < STAGES))
        def _():
            work(now)

        @pl.when(helper & (now >= 1) & (now <= STAGES))
        def _():
            relay(now - 1)

        @pl.when(t >= LAG)
        def _():
            finish(t - LAG)

        return 0

    lax.fori_loop(0, STAGES + LAG, tick, 0)

    def emf_copy(k):
        p = others(k)
        return pltpu.make_async_remote_copy(
            src_ref=acc.at[pl.ds(pl.multiple_of(p // 2 * 8, 8), 8), :], dst_ref=got.at[phi],
            send_sem=emf_send, recv_sem=emf_recv, device_id={"phi": p}, device_id_type=MESH)

    for k in range(1, PHI):
        emf_copy(k).start()
    pltpu.make_async_copy(acc.at[pl.ds(pl.multiple_of(phi // 2 * 8, 8), 8), :], got.at[phi], emf_recv).start()
    pltpu.make_async_copy(got, got, emf_recv).wait()
    summed = got[0]
    for p in range(1, PHI):
        summed = summed + got[p]
    summed = summed * (1.0 / NPHI)
    emf[...] = jnp.where(phi % 2 == 0, summed[:4], summed[4:])

    seven = got.at[pl.ds(0, 7)]
    drain(seven, emf_send)

    @pl.when(theta > 0)
    def _():
        theta_copy(0, theta).wait_send()

    @pl.when(theta < 7)
    def _():
        theta_copy(1, theta).wait_send()

    @pl.when(heavy)
    def _():
        keep_copy.wait_send()
        for n in range(ACROSS):
            drain(rx.at[0], across_send.at[n])

    @pl.when(source)
    def _():
        drain(rx.at[:, pl.ds(0, 7)], a_send)

    @pl.when(worker)
    def _():
        drain(yb.at[:, pl.ds(0, 7)], b_send)

    @pl.when(helper)
    def _():
        drain(rel, rel_send)

    def drain_out(n, _):
        out_copy(n).wait()
        return 0

    lax.fori_loop(0, STAGES, drain_out, 0)


def body(test_fields, velocity, kept):
    forward, inverse, singles, singles_back, modes = fourier_constants()
    tables = row_tables()
    hbm, vmem = pl.BlockSpec(memory_space=pltpu.HBM), pl.BlockSpec(memory_space=pltpu.VMEM)
    dma = pltpu.SemaphoreType.DMA
    result, emf = pl.pallas_call(
        kernel,
        out_shape=(
            jax.ShapeDtypeStruct((27, 4, 32, 256), F32),
            jax.ShapeDtypeStruct((4, 128), F32),
        ),
        in_specs=[hbm, hbm, vmem] + [hbm] * 6,
        out_specs=(hbm, vmem),
        scratch_shapes=[
            pltpu.VMEM((27, 4, 48, 256), F32),
            pltpu.VMEM((3, 4, 32, 256), F32),
            pltpu.VMEM((5, 32, 128), F32),
            pltpu.VMEM(forward.shape, BF16),
            pltpu.VMEM(inverse.shape, BF16),
            pltpu.VMEM(singles.shape, BF16),
            pltpu.VMEM(singles_back.shape, BF16),
            pltpu.VMEM(modes.shape, F32),
            pltpu.VMEM((2, 27, 4, 256), F32),
            pltpu.VMEM((2, 27, 4, 256), F32),
            pltpu.VMEM((27, 32, 256), F32),
            pltpu.VMEM((3, 4, 32, 256), F32),
            pltpu.VMEM((2, 32, 128), F32),
            pltpu.VMEM((27, 4, 32, 256), F32),
            pltpu.VMEM((STAGES, PHI, 3, 8, 256), F32),
            pltpu.VMEM((STAGES, PHI, 3, 8, 256), F32),
            pltpu.VMEM((27, 4, 32, 256), F32),
            pltpu.VMEM((STAGES, 3, 4, 16, 256), F32),
            pltpu.VMEM((32, 128), F32),
            pltpu.VMEM((PHI, 8, 128), F32),
            dma((8,)),
            dma((2,)),
            dma((2,)),
            dma((STAGES,)),
            dma((STAGES,)),
            dma,
            dma,
            dma,
            dma((ACROSS,)),
            dma((STAGES,)),
            dma,
            dma((STAGES,)),
            dma,
            dma((STAGES,)),
            dma((STAGES,)),
            dma,
            dma,
        ],
        compiler_params=pltpu.CompilerParams(
            collective_id=0, has_side_effects=True, vmem_limit_bytes=62 * 2**20
        ),
        name="substep",
    )(
        test_fields, velocity, kept.reshape(1, 32), jnp.asarray(tables), jnp.asarray(forward),
        jnp.asarray(inverse), jnp.asarray(singles), jnp.asarray(singles_back), jnp.asarray(modes),
    )
    emf = emf[:, :108].T.reshape(27, 4, 4)
    return result, emf


def solution(mesh):
    return jax.shard_map(
        body,
        mesh=mesh,
        in_specs=(P(None, "row", "theta", "phi"), P(None, "row", "theta", "phi"), P("theta")),
        out_specs=(P(None, "row", "theta", "phi"), P(None, "row", ("theta", "phi"))),
        check_vma=False,
    )
```

```python
import functools
import math

import jax
import jax.numpy as jnp
import ml_dtypes
import numpy as np
from jax import lax
from jax.experimental import pallas as pl
from jax.experimental.pallas import tpu as pltpu
from jax.sharding import PartitionSpec as P

MESH = pl.DeviceIdType.MESH
NPHI = 2048
MMAX = 512
STAGES = 9
AHEAD = 3
ELAG = 1
PIECES = ((0, 1), (1, 4), (4, 9))
ACROSS = 2
LAG = 12
BEHIND = 4
LIGHT_BEHIND = 4
HELP = 0
FAR = 0
VIA = 2
PLAN = ("FH", "OF", "OH", "FH", "OF", "OH", "OF", "OH", "OH")
FAR_WORK = (("L", 0), ("H", 0), ("H", 1), ("H", 3), ("H", 4), ("H", 6))
OWN = tuple(n for n in range(STAGES) if "O" in PLAN[n])
HELPED = tuple(n for n in range(STAGES) if "H" in PLAN[n])
FARRED = tuple(n for n in range(STAGES) if "F" in PLAN[n])
LIGHT_FAR = tuple(n for kind, n in FAR_WORK if kind == "L")
LIGHT_OWN = tuple(n for n in range(STAGES) if n not in LIGHT_FAR)
PHI = 8
F32 = jnp.float32
BF16 = jnp.bfloat16


def split_bf16(a):
    hi = a.astype(ml_dtypes.bfloat16)
    lo = (a - hi.astype(np.float64)).astype(ml_dtypes.bfloat16)
    return np.stack([hi, lo])


def fourier_constants():
    cell = np.arange(256)
    block = np.arange(64)

    def tables(mode):
        angle = 2.0 * math.pi * ((cell[:, None] * mode[None, :]) % NPHI) / NPHI
        return np.cos(angle), np.sin(angle)

    def scale(mode):
        return np.where(mode == 0, 1.0 / NPHI, 2.0 / NPHI)

    forward, inverse, modes = [], [], []
    singles, singles_back = [], []
    for r in (0, 4):
        mode = 8 * block + r
        c, s = tables(mode)
        full = np.concatenate([c, s], axis=1)
        singles.append(full)
        singles_back.append((full * np.tile(scale(mode), 2)).T)
        modes.append(np.tile(mode, 2))
    modes = [np.concatenate(modes)]
    for r in (1, 2, 3):
        m, n = 8 * block + r, 8 * block + 8 - r
        cm, sm = tables(m)
        cn, sn = tables(n)
        upper = np.concatenate([cm, sm, cn, sn], axis=1)
        lower = np.concatenate([-sm, cm, sn, -cn], axis=1)
        full = np.concatenate([upper, lower], axis=0)
        weights = np.concatenate([scale(m), scale(m), scale(n), scale(n)])
        forward.append(full)
        inverse.append((full * weights).T)
        modes.append(np.concatenate([m, m, n, n]))
    modes = np.broadcast_to(np.stack(modes).astype(np.float32)[:, None, :], (4, 8, 256))
    return (
        split_bf16(np.stack(forward)),
        split_bf16(np.stack(inverse)),
        split_bf16(np.stack(singles)),
        split_bf16(np.stack(singles_back)),
        np.ascontiguousarray(modes),
    )


def row_tables():
    j = np.arange(256)
    d = math.pi / 256
    angle = d * (j + 0.5)
    south = np.sin(angle + 0.5 * d) / np.sin(angle)
    north = np.sin(angle - 0.5 * d) / np.sin(angle)
    polar = (3 * (2 * j + 1) < 256) | (3 * (2 * (255 - j) + 1) < 256)
    kinds = np.stack([south, north, np.cos(angle), np.sin(angle), polar.astype(np.float64)])
    kinds = kinds.reshape(5, 8, 32).transpose(1, 0, 2)
    return np.ascontiguousarray(np.broadcast_to(kinds[..., None], (8, 5, 32, 128)).astype(np.float32))


def radial_constants():
    h = 0.3 / 8
    r = 0.7 + h * (np.arange(8) + 0.5)
    return ((r + h / 2) / r) ** 2, ((r - h / 2) / r) ** 2, (1.0 / r) ** 2


def split_rows(a):
    hi = a.astype(BF16).astype(F32)
    return jnp.concatenate([hi, a - hi], axis=0).astype(BF16)


def dot(a, b):
    return jnp.dot(a, b, preferred_element_type=F32)


def dot_split(a, high, low):
    lines = a.shape[0]
    both = split_rows(a)
    out = dot(both, high) + dot(both, low)
    return out[:lines] + out[lines:]


def filter_lines(blocks, keep, modes, fwd, inv, one, back):
    x0, x1, x2, x3, x4, x5, x6, x7 = blocks
    half = math.sqrt(0.5)
    s04, d04, s26, d26 = x0 + x4, x0 - x4, x2 + x6, x2 - x6
    s15, d15, s37, d37 = x1 + x5, x1 - x5, x3 + x7, x3 - x7
    even, odd = s04 + s26, s15 + s37
    cross, plus = half * (d15 - d37), half * (d15 + d37)
    pairs = [(d04 + cross, d26 + plus), (s04 - s26, s15 - s37), (d04 - cross, plus - d26)]

    def masked(mid, group):
        lines = mid.shape[0]
        kept = mid.reshape(lines // 8, 8, 256)
        kept = jnp.where((modes[group] < keep)[None], kept, 0.0)
        return kept.reshape(lines, 256)

    mid = jnp.concatenate(
        [dot_split(even + odd, one[0, 0], one[1, 0]), dot_split(even - odd, one[0, 1], one[1, 1])], axis=1
    )
    mid = masked(mid, 0)
    p0 = dot_split(mid[:, :128], back[0, 0], back[1, 0])
    p4 = dot_split(mid[:, 128:], back[0, 1], back[1, 1])
    p, q = [], []
    for r, (u, v) in enumerate(pairs):
        mid = dot_split(jnp.concatenate([u, v], axis=1), fwd[0, r], fwd[1, r])
        mid = masked(mid, r + 1)
        out = dot_split(mid, inv[0, r], inv[1, r])
        p.append(out[:, :256])
        q.append(out[:, 256:])
    (p1, p2, p3), (q1, q2, q3) = p, q
    a, b = p0 + p4, p0 - p4
    p13, q13 = p1 + p3, q1 - q3
    ph, qh = half * (p1 - p3), half * (q1 + q3)
    ap, am, bp, bm = a + p2, a - p2, b + q2, b - q2
    return [
        ap + p13,
        bp + (ph + qh),
        am + q13,
        bm - (ph - qh),
        ap - p13,
        bp - (ph + qh),
        am - q13,
        bm + (ph - qh),
    ]


def member(n, values):
    found = n == values[0]
    for value in values[1:]:
        found = found | (n == value)
    return found


def rank(n, values):
    return sum(jnp.where(n > value, 1, 0) for value in values)


def pick(n, values):
    out = values[0]
    for k in range(1, len(values)):
        out = jnp.where(n >= k, values[k], out)
    return out


def kernel(
    tf, vel, kept_hbm, tab_hbm, fwd_hbm, inv_hbm, one_hbm, back_hbm, modes_hbm,
    res, emf,
    xp, v, kept, tab, fwd, inv, one, back, modes,
    edge, halo_t, halo_r, coef, radius, keep, mask, st, rx, yb, rel, vb, acc, got,
    load_sem, theta_send, theta_recv, row_send, row_recv, keep_send, keep_recv,
    a_send, across_send, via_send, via_recv, far_send, a_recv, b_send, b_recv, rel_send, rel_recv, emf_send, emf_recv,
):
    phi, theta, row = lax.axis_index("phi"), lax.axis_index("theta"), lax.axis_index("row")
    group = theta % 2
    heavy_at, helper_at, far_at, light_at = 7 * group, 2 + 3 * group, 4 - group, 6 - 5 * group
    heavy, helper, far, light = theta == heavy_at, theta == helper_at, theta == far_at, theta == light_at
    source = heavy | light
    light_octet = 2 - 2 * group
    octet = jnp.where(light, light_octet, 0)
    my_i, my_half = phi // 2, phi % 2
    edge_i, main_i = 3 - 3 * row, row
    late = jnp.where(my_i == edge_i, ELAG, 0)

    def others(k):
        return lax.rem(phi + k, PHI)

    loads = [
        pltpu.make_async_copy(tf, xp.at[:, :, pl.ds(8, 32), :], load_sem.at[0]),
        pltpu.make_async_copy(vel, v, load_sem.at[1]),
        pltpu.make_async_copy(tab_hbm.at[theta], tab, load_sem.at[2]),
        pltpu.make_async_copy(fwd_hbm, fwd, load_sem.at[3]),
        pltpu.make_async_copy(inv_hbm, inv, load_sem.at[4]),
        pltpu.make_async_copy(one_hbm, one, load_sem.at[5]),
        pltpu.make_async_copy(back_hbm, back, load_sem.at[6]),
        pltpu.make_async_copy(modes_hbm, modes, load_sem.at[7]),
        pltpu.make_async_copy(tab_hbm.at[jnp.where(far, light_at, theta), 4], mask, load_sem.at[8]),
        pltpu.make_async_copy(kept_hbm, kept, load_sem.at[9]),
    ]
    for load in loads:
        load.start()

    barrier = pltpu.get_barrier_semaphore()
    pl.semaphore_signal(barrier, inc=1, device_id={"row": 1 - row}, device_id_type=MESH)
    for k in range(1, PHI):
        pl.semaphore_signal(barrier, inc=1, device_id={"phi": others(k)}, device_id_type=MESH)

    @pl.when(theta > 0)
    def _():
        pl.semaphore_signal(barrier, inc=1, device_id={"theta": theta - 1}, device_id_type=MESH)

    @pl.when(theta < 7)
    def _():
        pl.semaphore_signal(barrier, inc=1, device_id={"theta": theta + 1}, device_id_type=MESH)

    def greet_all(there):
        for k in range(PHI):
            pl.semaphore_signal(barrier, inc=1, device_id={"theta": there, "phi": others(k)}, device_id_type=MESH)

    def greet(there):
        pl.semaphore_signal(barrier, inc=1, device_id={"theta": there}, device_id_type=MESH)

    @pl.when(heavy)
    def _():
        greet_all(helper_at)
        greet(far_at)
        greet(light_at)

    @pl.when(helper)
    def _():
        greet_all(heavy_at)

    @pl.when(far)
    def _():
        greet_all(light_at)
        greet(heavy_at)

    @pl.when(light)
    def _():
        greet_all(far_at)
        greet(heavy_at)

    loads[0].wait()

    def pack(f, _):
        for i in range(4):
            edge[0, f, pl.ds(i, 1), :] = xp[f, i, pl.ds(8, 1), :]
            edge[1, f, pl.ds(i, 1), :] = xp[f, i, pl.ds(39, 1), :]
        return 0

    lax.fori_loop(0, 27, pack, 0)
    loads[9].wait()
    eye = lax.broadcasted_iota(jnp.int32, (32, 32), 0) == lax.broadcasted_iota(jnp.int32, (32, 32), 1)
    counts = jnp.where(eye, jnp.broadcast_to(kept[...], (32, 32)), 0).astype(F32)
    keep[0] = jnp.broadcast_to(jnp.sum(counts, axis=1, keepdims=True), (32, 128))

    peers = PHI + jnp.where(theta > 0, 1, 0) + jnp.where(theta < 7, 1, 0) + PHI
    peers = peers + jnp.where(heavy, 2, 0) + jnp.where(far | light, 1, 0)
    pl.semaphore_wait(barrier, peers)

    def theta_copy(n, side, there):
        first, last = PIECES[n]
        part = pl.ds(3 * first, 3 * (last - first))
        return pltpu.make_async_remote_copy(
            src_ref=edge.at[side, part], dst_ref=halo_t.at[side, part], send_sem=theta_send.at[side, n],
            recv_sem=theta_recv.at[side, n], device_id={"theta": there}, device_id_type=MESH)


    def row_copy(n):
        return pltpu.make_async_remote_copy(
            src_ref=xp.at[pl.ds(3 * n, 3), edge_i, pl.ds(8, 32), :], dst_ref=halo_r.at[pl.ds(3 * n, 3)],
            send_sem=row_send.at[n], recv_sem=row_recv.at[n],
            device_id={"row": 1 - row}, device_id_type=MESH)

    def send_theta(n):
        @pl.when(theta > 0)
        def _():
            theta_copy(n, 0, theta - 1).start()

        @pl.when(theta < 7)
        def _():
            theta_copy(n, 1, theta + 1).start()

    def wait_theta(n):
        @pl.when(theta > 0)
        def _():
            theta_copy(n, 0, theta).wait_send()
            theta_copy(n, 1, theta).wait_recv()

        @pl.when(theta < 7)
        def _():
            theta_copy(n, 1, theta).wait_send()
            theta_copy(n, 0, theta).wait_recv()

    send_theta(0)
    row_copy(0).start()
    send_theta(1)
    for n in range(1, AHEAD):
        row_copy(n).start()

    def keep_copy(slot, sem, there):
        return pltpu.make_async_remote_copy(
            src_ref=keep.at[0], dst_ref=keep.at[slot], send_sem=keep_send.at[sem], recv_sem=keep_recv.at[slot - 1],
            device_id={"theta": there}, device_id_type=MESH)

    @pl.when(heavy)
    def _():
        keep_copy(1, 0, helper_at).start()
        keep_copy(1, 1, far_at).start()

    @pl.when(light)
    def _():
        keep_copy(2, 0, far_at).start()

    for load in loads[1:9]:
        load.wait()
    outward, inward, metric = radial_constants()

    def radial(values, i):
        return jnp.where(row == 0, F32(values[i]), F32(values[i + 4]))

    for i in range(4):
        radius[0, i] = 0.2 * radial(outward, i) * (1.0 if i < 3 else jnp.where(row == 0, F32(1.0), F32(0.0)))
        radius[1, i] = 0.2 * radial(inward, i) * (1.0 if i > 0 else jnp.where(row == 1, F32(1.0), F32(0.0)))

    south, north = tab[0], tab[1]
    for i in range(4):
        g = 0.1 * radial(metric, i)
        cs, cn = g * south, g * north
        both = 0.2 * (radial(outward, i) + radial(inward, i))
        centre = (1.0 - both) - (cs + cn)
        for lanes in range(2):
            part = pl.ds(128 * lanes, 128)
            coef[0, i, :, part] = cs
            coef[1, i, :, part] = cn
            coef[2, i, :, part] = centre

    @pl.when(theta == 7)
    def _():
        halo_t[0] = jnp.zeros((27, 4, 256), F32)

    @pl.when(theta == 0)
    def _():
        halo_t[1] = jnp.zeros((27, 4, 256), F32)

    def drain(ref, sem):
        pltpu.make_async_copy(ref, ref, sem).wait()

    def chunk(n, p, rows):
        return st.at[pl.ds(3 * n, 3), p // 2, pl.ds(pl.multiple_of((rows + p % 2) * 8, 8), 8), :]

    def a_copy(n, p, there, rows, slot, sem):
        return pltpu.make_async_remote_copy(
            src_ref=chunk(n, p, rows), dst_ref=rx.at[slot, phi], send_sem=sem, recv_sem=a_recv.at[slot],
            device_id={"theta": there, "phi": p}, device_id_type=MESH)

    main_workers = [2 * main_i + lax.rem(phi + q, 6) for q in range(6)]
    edge_workers = [2 * edge_i + lax.rem(phi + q, 2) for q in range(2)]

    def far_octet(n):
        return jnp.where(member(n, OWN), 2, 0)

    def via_copy(n, part):
        r = rank(n, FARRED)
        layers = pl.ds(main_i, 3) if part == 0 else pl.ds(edge_i, 1)
        return pltpu.make_async_remote_copy(
            src_ref=st.at[pl.ds(3 * n, 3), layers, pl.ds(pl.multiple_of(far_octet(n) * 8, 8), 16), :],
            dst_ref=vb.at[r, :, layers], send_sem=via_send.at[part, lax.rem(r, ACROSS)],
            recv_sem=via_recv.at[part, r], device_id={"theta": light_at}, device_id_type=MESH)

    def pass_on(r, part):
        got_part = vb.at[r, :, pl.ds(main_i, 3)] if part == 0 else vb.at[r, :, pl.ds(edge_i, 1)]
        pltpu.make_async_copy(got_part, got_part, via_recv.at[part, r]).wait()
        slot = pick(r, [k for k, (kind, _) in enumerate(FAR_WORK) if kind == "H"])
        for p in main_workers if part == 0 else edge_workers:
            pltpu.make_async_remote_copy(
                src_ref=vb.at[r, :, p // 2, pl.ds(pl.multiple_of(p % 2 * 8, 8), 8), :],
                dst_ref=rx.at[slot, phi], send_sem=far_send, recv_sem=a_recv.at[slot],
                device_id={"theta": far_at, "phi": p}, device_id_type=MESH,
            ).start()

    def layer(n, i, neighbours):
        p_unit, q_unit = n // 3, n % 3
        unit = [jnp.where(p_unit == k, F32(0.5), F32(0.0)) for k in range(3)]
        weight = [jnp.where(q_unit == k, F32(1.0), F32(0.0)) for k in range(3)]
        profile = weight[0] + weight[1] * tab[2] + weight[2] * tab[3]
        profile = jnp.concatenate([profile, profile], axis=1)
        v0, v1, v2 = v[0, i], v[1, i], v[2, i]
        turned = (v1 * unit[2] - v2 * unit[1], v2 * unit[0] - v0 * unit[2], v0 * unit[1] - v1 * unit[0])
        for c in range(3):
            f = 3 * n + c
            xp[f, i, pl.ds(7, 1), :] = halo_t[1, f, pl.ds(i, 1), :]
            xp[f, i, pl.ds(40, 1), :] = halo_t[0, f, pl.ds(i, 1), :]
            total = coef[2, i] * xp[f, i, pl.ds(8, 32), :] + profile * turned[c]
            for factor, other in neighbours(f):
                total = total + factor * other
            total = total + coef[0, i] * xp[f, i, pl.ds(9, 32), :] + coef[1, i] * xp[f, i, pl.ds(7, 32), :]
            st[f, i] = total

        @pl.when(light)
        def _():
            rest = pl.ds(pl.multiple_of(16 - 8 * light_octet, 8), 16)
            for c in range(3):
                res[3 * n + c, i, rest, :] = st[3 * n + c, i, rest, :]

        @pl.when(jnp.logical_not(source))
        def _():
            for c in range(3):
                res[3 * n + c, i] = st[3 * n + c, i]

    def send(n, part):
        workers = main_workers if part == 0 else edge_workers

        @pl.when((heavy & member(n, OWN)) | (light & member(n, LIGHT_OWN)))
        def _():
            for p in workers:

                @pl.when(p == phi)
                def _(p=p):
                    pltpu.make_async_copy(chunk(n, p, octet), rx.at[n, phi], a_recv.at[n]).start()

                @pl.when(p != phi)
                def _(p=p):
                    a_copy(n, p, theta, octet, n, a_send).start()

        @pl.when(light & member(n, LIGHT_FAR))
        def _():
            slot = pick(rank(n, LIGHT_FAR), [k for k, (kind, _) in enumerate(FAR_WORK) if kind == "L"])
            for p in workers:
                a_copy(n, p, far_at, octet, slot, far_send).start()

        @pl.when(heavy & member(n, FARRED))
        def _():
            @pl.when(rank(n, FARRED) >= ACROSS)
            def _():
                via_copy(n, part).wait_send()

            via_copy(n, part).start()

        @pl.when(heavy & member(n, HELPED))
        def _():
            r = rank(n, HELPED)
            sem = across_send.at[part, lax.rem(r, ACROSS)]

            @pl.when(r >= ACROSS)
            def _():
                drain(rx.at[0, pl.ds(0, len(workers))], sem)

            for p in workers:
                a_copy(n, p, helper_at, 2, n, sem).start()

    def step_main(n):
        for k, (first, _) in enumerate(PIECES):

            @pl.when(n == first)
            def _(k=k):
                wait_theta(k)

        @pl.when(n == 0)
        def _():
            send_theta(2)

        for m in range(3):
            i = main_i + m

            def neighbours(f, i=i):
                up, down = jnp.minimum(i + 1, 3), jnp.maximum(i - 1, 0)
                return (
                    (radius[0, i], xp[f, up, pl.ds(8, 32), :]),
                    (radius[1, i], xp[f, down, pl.ds(8, 32), :]),
                )

            layer(n, i, neighbours)
        send(n, 0)

    def step_edge(n):
        row_copy(n).wait_recv()
        row_copy(n).wait_send()

        @pl.when(n + AHEAD < STAGES)
        def _():
            row_copy(n + AHEAD).start()

        def neighbours(f):
            return (
                (radius[row, edge_i], halo_r[f]),
                (radius[1 - row, edge_i], xp[f, 2 - row, pl.ds(8, 32), :]),
            )

        layer(n, edge_i, neighbours)
        send(n, 1)

    half_rows = pl.ds(pl.multiple_of(my_half * 8, 8), 8)

    def b_copy(n, p):
        return pltpu.make_async_remote_copy(
            src_ref=yb.at[n, p],
            dst_ref=res.at[pl.ds(3 * n, 3), my_i, pl.ds(pl.multiple_of((octet + my_half) * 8, 8), 8), :],
            send_sem=b_send, recv_sem=b_recv.at[n],
            device_id={"phi": p}, device_id_type=MESH)

    def gather_copy(slot, p):
        return pltpu.make_async_remote_copy(
            src_ref=yb.at[slot, p], dst_ref=rel.at[slot, :, my_i, half_rows, :],
            send_sem=b_send, recv_sem=rel_recv.at[slot], device_id={"phi": p}, device_id_type=MESH)

    far_light = [1 if kind == "L" else 0 for kind, _ in FAR_WORK]
    far_stage = [n for _, n in FAR_WORK]

    def relay(slot):
        pltpu.make_async_copy(rel.at[slot], rel.at[slot], rel_recv.at[slot]).wait()
        to_light = far & (pick(slot, far_light) == 1)
        n = jnp.where(far, pick(slot, far_stage), slot)
        rows = jnp.where(to_light, light_octet, jnp.where(far, far_octet(n), 2))
        pltpu.make_async_remote_copy(
            src_ref=rel.at[slot],
            dst_ref=res.at[pl.ds(3 * n, 3), :, pl.ds(pl.multiple_of(rows * 8, 8), 16), :],
            send_sem=rel_send, recv_sem=b_recv.at[n],
            device_id={"theta": jnp.where(to_light, light_at, heavy_at)}, device_id_type=MESH,
        ).start()

    def work(slot):
        @pl.when((helper & (slot == HELPED[0])) | (far & (slot == 0)))
        def _():
            keep_copy(1, 0, theta).wait_recv()

        @pl.when(far & (slot == 0))
        def _():
            keep_copy(2, 0, theta).wait_recv()

        on_light = far & (pick(slot, far_light) == 1)
        far_rows = jnp.where(on_light, light_octet, far_octet(pick(slot, far_stage)))
        rows = jnp.where(far, far_rows, jnp.where(helper, 2, octet)) + my_half
        mine = pl.ds(pl.multiple_of(rows * 8, 8), 8)
        kept_rows = keep[jnp.where(on_light, 2, jnp.where(source, 0, 1)), mine, :]
        kept_rows = jnp.concatenate([kept_rows, kept_rows], axis=1)
        polar = jnp.maximum(mask[mine, :], jnp.where(light | on_light, F32(0.0), F32(1.0)))
        polar = jnp.concatenate([polar, polar], axis=1) > 0.5
        pltpu.make_async_copy(rx.at[slot], rx.at[slot], a_recv.at[slot]).wait()
        blocks = [rx[slot, p].reshape(24, 256) for p in range(PHI)]
        done = filter_lines(blocks, kept_rows, modes, fwd, inv, one, back)
        for p in range(PHI):
            yb[slot, p] = jnp.where(polar[None], done[p].reshape(3, 8, 256), rx[slot, p])

        @pl.when(source)
        def _():
            pltpu.make_async_copy(
                yb.at[slot, phi], res.at[pl.ds(3 * slot, 3), my_i, mine, :], b_recv.at[slot]
            ).start()
            for k in range(1, PHI):
                b_copy(slot, others(k)).start()

        @pl.when(jnp.logical_not(source))
        def _():
            pltpu.make_async_copy(
                yb.at[slot, phi], rel.at[slot, :, my_i, half_rows, :], rel_recv.at[slot]
            ).start()
            for k in range(1, PHI):
                gather_copy(slot, others(k)).start()

    acc[...] = jnp.zeros((32, 128), F32)
    lane = lax.broadcasted_iota(jnp.int32, (32, 128), 1)

    def finish(n):
        @pl.when(heavy)
        def _():
            whole = res.at[pl.ds(3 * n, 3)]
            pltpu.make_async_copy(whole, whole, b_recv.at[n]).wait()

        @pl.when(light)
        def _():
            part = res.at[pl.ds(3 * n, 3), :, pl.ds(pl.multiple_of(octet * 8, 8), 16), :]
            pltpu.make_async_copy(part, part, b_recv.at[n]).wait()

        total = acc[...]
        for i in range(4):
            v0, v1, v2 = v[0, i], v[1, i], v[2, i]
            r0, r1, r2 = res[3 * n, i], res[3 * n + 1, i], res[3 * n + 2, i]
            terms = (v1 * r2 - v2 * r1, v2 * r0 - v0 * r2, v0 * r1 - v1 * r0)
            for c in range(3):
                summed = jnp.sum(terms[c][:, :128] + terms[c][:, 128:], axis=1, keepdims=True)
                total = jnp.where(lane == 27 * i + 3 * n + c, jnp.broadcast_to(summed, (32, 128)), total)
        acc[...] = total

    def tick(t, _):
        @pl.when(t < STAGES)
        def _():
            step_main(t)

        @pl.when((t >= ELAG) & (t < STAGES + ELAG))
        def _():
            step_edge(t - ELAG)

        for part in range(2):
            first = VIA + ELAG * part

            @pl.when(light & (t >= first) & (t < first + len(FARRED)))
            def _(part=part, first=first):
                pass_on(t - first, part)

        def busy(slot):
            mine = (heavy & member(slot, OWN)) | (light & member(slot, LIGHT_OWN))
            theirs = (helper & member(slot, HELPED)) | (far & (slot >= 0) & (slot < len(FAR_WORK)))
            return mine | theirs

        at = t - jnp.where(helper, HELP, jnp.where(far, FAR, jnp.where(light, LIGHT_BEHIND, BEHIND)))

        @pl.when(busy(at - late))
        def _():
            work(at - late)

        @pl.when((helper | far) & busy(at - ELAG - 1))
        def _():
            relay(at - ELAG - 1)

        @pl.when(t >= LAG)
        def _():
            finish(t - LAG)

        return 0

    lax.fori_loop(0, STAGES + LAG, tick, 0)

    def emf_copy(k):
        p = others(k)
        return pltpu.make_async_remote_copy(
            src_ref=acc.at[pl.ds(pl.multiple_of(p // 2 * 8, 8), 8), :], dst_ref=got.at[phi],
            send_sem=emf_send, recv_sem=emf_recv, device_id={"phi": p}, device_id_type=MESH)

    for k in range(1, PHI):
        emf_copy(k).start()
    pltpu.make_async_copy(acc.at[pl.ds(pl.multiple_of(phi // 2 * 8, 8), 8), :], got.at[phi], emf_recv).start()
    pltpu.make_async_copy(got, got, emf_recv).wait()
    summed = got[0]
    for p in range(1, PHI):
        summed = summed + got[p]
    summed = summed * (1.0 / NPHI)
    mean = jnp.where(phi % 2 == 0, summed[:4], summed[4:])
    for i in range(4):
        emf[i] = mean[:, 27 * i : 27 * i + 27]

    seven = got.at[pl.ds(0, 7)]
    drain(seven, emf_send)

    @pl.when(heavy)
    def _():
        keep_copy(1, 0, theta).wait_send()
        keep_copy(1, 1, theta).wait_send()
        for n in range(ACROSS):
            drain(rx.at[0, pl.ds(0, 6)], across_send.at[0, n])
            drain(rx.at[0, pl.ds(0, 2)], across_send.at[1, n])
            drain(vb.at[0, :, pl.ds(0, 3)], via_send.at[0, n])
            drain(vb.at[0, :, pl.ds(0, 1)], via_send.at[1, n])
        drain(rx.at[pl.ds(0, len(OWN)), pl.ds(0, 7)], a_send)
        drain(yb.at[pl.ds(0, len(OWN)), pl.ds(0, 7)], b_send)

    @pl.when(light)
    def _():
        keep_copy(2, 0, theta).wait_send()
        drain(rx.at[pl.ds(0, len(LIGHT_OWN)), pl.ds(0, 7)], a_send)
        drain(yb.at[pl.ds(0, len(LIGHT_OWN)), pl.ds(0, 7)], b_send)
        drain(rx.at[pl.ds(0, len(FAR_WORK))], far_send)

    @pl.when(helper)
    def _():
        drain(yb.at[pl.ds(0, len(HELPED)), pl.ds(0, 7)], b_send)
        drain(rel.at[pl.ds(0, len(HELPED))], rel_send)

    @pl.when(far)
    def _():
        drain(yb.at[pl.ds(0, len(FAR_WORK)), pl.ds(0, 7)], b_send)
        drain(rel.at[pl.ds(0, len(FAR_WORK))], rel_send)


def body(test_fields, velocity, kept):
    forward, inverse, singles, singles_back, modes = fourier_constants()
    tables = row_tables()
    hbm, vmem = pl.BlockSpec(memory_space=pltpu.HBM), pl.BlockSpec(memory_space=pltpu.VMEM)
    dma = pltpu.SemaphoreType.DMA
    result, emf = pl.pallas_call(
        kernel,
        out_shape=(
            jax.ShapeDtypeStruct((27, 4, 32, 256), F32),
            jax.ShapeDtypeStruct((4, 4, 27), F32),
        ),
        in_specs=[hbm] * 9,
        out_specs=(vmem, vmem),
        scratch_shapes=[
            pltpu.VMEM((27, 4, 48, 256), F32),
            pltpu.VMEM((3, 4, 32, 256), F32),
            pltpu.VMEM((1, 32), jnp.int32),
            pltpu.VMEM((5, 32, 128), F32),
            pltpu.VMEM(forward.shape, BF16),
            pltpu.VMEM(inverse.shape, BF16),
            pltpu.VMEM(singles.shape, BF16),
            pltpu.VMEM(singles_back.shape, BF16),
            pltpu.VMEM(modes.shape, F32),
            pltpu.VMEM((2, 27, 4, 256), F32),
            pltpu.VMEM((2, 27, 4, 256), F32),
            pltpu.VMEM((27, 32, 256), F32),
            pltpu.VMEM((3, 4, 32, 256), F32),
            pltpu.SMEM((2, 4), F32),
            pltpu.VMEM((3, 32, 128), F32),
            pltpu.VMEM((32, 128), F32),
            pltpu.VMEM((27, 4, 32, 256), F32),
            pltpu.VMEM((STAGES, PHI, 3, 8, 256), F32),
            pltpu.VMEM((STAGES, PHI, 3, 8, 256), F32),
            pltpu.VMEM((STAGES, 3, 4, 16, 256), F32),
            pltpu.VMEM((len(FARRED), 3, 4, 16, 256), F32),
            pltpu.VMEM((32, 128), F32),
            pltpu.VMEM((PHI, 8, 128), F32),
            dma((10,)),
            dma((2, len(PIECES))),
            dma((2, len(PIECES))),
            dma((STAGES,)),
            dma((STAGES,)),
            dma((2,)),
            dma((2,)),
            dma,
            dma((2, ACROSS)),
            dma((2, ACROSS)),
            dma((2, len(FARRED))),
            dma,
            dma((STAGES,)),
            dma,
            dma((STAGES,)),
            dma,
            dma((STAGES,)),
            dma,
            dma,
        ],
        compiler_params=pltpu.CompilerParams(
            collective_id=0, has_side_effects=True, vmem_limit_bytes=40 * 2**20
        ),
        name="substep",
    )(
        *(
            pltpu.with_memory_space_constraint(jnp.asarray(a), pltpu.HBM)
            for a in (
                test_fields, velocity, kept.reshape(1, 32), tables, forward, inverse, singles, singles_back, modes,
            )
        )
    )
    return result, jnp.transpose(emf, (2, 0, 1))


def solution(mesh):
    return jax.shard_map(
        body,
        mesh=mesh,
        in_specs=(P(None, "row", "theta", "phi"), P(None, "row", "theta", "phi"), P("theta")),
        out_specs=(P(None, "row", "theta", "phi"), P(None, "row", ("theta", "phi"))),
        check_vma=False,
    )
```

```python
import functools
import math

import jax
import jax.numpy as jnp
import ml_dtypes
import numpy as np
from jax import lax
from jax.experimental import pallas as pl
from jax.experimental.pallas import tpu as pltpu
from jax.sharding import PartitionSpec as P

MESH = pl.DeviceIdType.MESH
NPHI = 2048
MMAX = 512
STAGES = 9
AHEAD = 3
ELAG = 1
PIECES = ((0, 1), (1, 3), (3, 5), (5, 7), (7, 9))
ACROSS = 2
LAG = 12
BEHIND = 4
LIGHT_BEHIND = 4
HELP = 0
FAR = 0
VIA = 2
PLAN = ("FH", "OF", "OH", "FH", "OF", "OH", "OH", "OO", "OH")
FAR_WORK = (("L", 0), ("H", 0), ("H", 1), ("H", 3), ("H", 4))
OWN = tuple(n for n in range(STAGES) if "O" in PLAN[n])
DOUBLE = PLAN.index("OO")
SECOND = STAGES
HELPED = tuple(n for n in range(STAGES) if "H" in PLAN[n])
FARRED = tuple(n for n in range(STAGES) if "F" in PLAN[n])
LIGHT_FAR = tuple(n for kind, n in FAR_WORK if kind == "L")
LIGHT_OWN = tuple(n for n in range(STAGES) if n not in LIGHT_FAR)
PHI = 8
F32 = jnp.float32
BF16 = jnp.bfloat16


def split_bf16(a):
    hi = a.astype(ml_dtypes.bfloat16)
    lo = (a - hi.astype(np.float64)).astype(ml_dtypes.bfloat16)
    return np.stack([hi, lo])


def fourier_constants():
    cell = np.arange(256)
    block = np.arange(64)

    def tables(mode):
        angle = 2.0 * math.pi * ((cell[:, None] * mode[None, :]) % NPHI) / NPHI
        return np.cos(angle), np.sin(angle)

    def scale(mode):
        return np.where(mode == 0, 1.0 / NPHI, 2.0 / NPHI)

    forward, inverse, modes = [], [], []
    singles, singles_back = [], []
    for r in (0, 4):
        mode = 8 * block + r
        c, s = tables(mode)
        full = np.concatenate([c, s], axis=1)
        singles.append(full)
        singles_back.append((full * np.tile(scale(mode), 2)).T)
        modes.append(np.tile(mode, 2))
    modes = [np.concatenate(modes)]
    for r in (1, 2, 3):
        m, n = 8 * block + r, 8 * block + 8 - r
        cm, sm = tables(m)
        cn, sn = tables(n)
        upper = np.concatenate([cm, sm, cn, sn], axis=1)
        lower = np.concatenate([-sm, cm, sn, -cn], axis=1)
        full = np.concatenate([upper, lower], axis=0)
        weights = np.concatenate([scale(m), scale(m), scale(n), scale(n)])
        forward.append(full)
        inverse.append((full * weights).T)
        modes.append(np.concatenate([m, m, n, n]))
    modes = np.broadcast_to(np.stack(modes).astype(np.float32)[:, None, :], (4, 8, 256))
    return (
        split_bf16(np.stack(forward)),
        split_bf16(np.stack(inverse)),
        split_bf16(np.stack(singles)),
        split_bf16(np.stack(singles_back)),
        np.ascontiguousarray(modes),
    )


def row_tables():
    j = np.arange(256)
    d = math.pi / 256
    angle = d * (j + 0.5)
    south = np.sin(angle + 0.5 * d) / np.sin(angle)
    north = np.sin(angle - 0.5 * d) / np.sin(angle)
    polar = (3 * (2 * j + 1) < 256) | (3 * (2 * (255 - j) + 1) < 256)
    kinds = np.stack([south, north, np.cos(angle), np.sin(angle), polar.astype(np.float64)])
    kinds = kinds.reshape(5, 8, 32).transpose(1, 0, 2)
    return np.ascontiguousarray(np.broadcast_to(kinds[..., None], (8, 5, 32, 128)).astype(np.float32))


def radial_constants():
    h = 0.3 / 8
    r = 0.7 + h * (np.arange(8) + 0.5)
    return ((r + h / 2) / r) ** 2, ((r - h / 2) / r) ** 2, (1.0 / r) ** 2


def split_rows(a):
    hi = a.astype(BF16).astype(F32)
    return jnp.concatenate([hi, a - hi], axis=0).astype(BF16)


def dot(a, b):
    return jnp.dot(a, b, preferred_element_type=F32)


def dot_split(a, high, low):
    lines = a.shape[0]
    both = split_rows(a)
    out = dot(both, high) + dot(both, low)
    return out[:lines] + out[lines:]


def filter_lines(blocks, keep, modes, fwd, inv, one, back):
    x0, x1, x2, x3, x4, x5, x6, x7 = blocks
    half = math.sqrt(0.5)
    s04, d04, s26, d26 = x0 + x4, x0 - x4, x2 + x6, x2 - x6
    s15, d15, s37, d37 = x1 + x5, x1 - x5, x3 + x7, x3 - x7
    even, odd = s04 + s26, s15 + s37
    cross, plus = half * (d15 - d37), half * (d15 + d37)
    pairs = [(d04 + cross, d26 + plus), (s04 - s26, s15 - s37), (d04 - cross, plus - d26)]

    def masked(mid, group):
        lines = mid.shape[0]
        kept = mid.reshape(lines // 8, 8, 256)
        kept = jnp.where((modes[group] < keep)[None], kept, 0.0)
        return kept.reshape(lines, 256)

    mid = jnp.concatenate(
        [dot_split(even + odd, one[0, 0], one[1, 0]), dot_split(even - odd, one[0, 1], one[1, 1])], axis=1
    )
    mid = masked(mid, 0)
    p0 = dot_split(mid[:, :128], back[0, 0], back[1, 0])
    p4 = dot_split(mid[:, 128:], back[0, 1], back[1, 1])
    p, q = [], []
    for r, (u, v) in enumerate(pairs):
        mid = dot_split(jnp.concatenate([u, v], axis=1), fwd[0, r], fwd[1, r])
        mid = masked(mid, r + 1)
        out = dot_split(mid, inv[0, r], inv[1, r])
        p.append(out[:, :256])
        q.append(out[:, 256:])
    (p1, p2, p3), (q1, q2, q3) = p, q
    a, b = p0 + p4, p0 - p4
    p13, q13 = p1 + p3, q1 - q3
    ph, qh = half * (p1 - p3), half * (q1 + q3)
    ap, am, bp, bm = a + p2, a - p2, b + q2, b - q2
    return [
        ap + p13,
        bp + (ph + qh),
        am + q13,
        bm - (ph - qh),
        ap - p13,
        bp - (ph + qh),
        am - q13,
        bm + (ph - qh),
    ]


def member(n, values):
    found = n == values[0]
    for value in values[1:]:
        found = found | (n == value)
    return found


def rank(n, values):
    return sum(jnp.where(n > value, 1, 0) for value in values)


def pick(n, values):
    out = values[0]
    for k in range(1, len(values)):
        out = jnp.where(n >= k, values[k], out)
    return out


def kernel(
    tf, vel, kept_hbm, tab_hbm, fwd_hbm, inv_hbm, one_hbm, back_hbm, modes_hbm,
    res, emf,
    xp, v, kept, tab, fwd, inv, one, back, modes,
    edge, halo_t, halo_r, coef, radius, keep, mask, st, rx, yb, rel, vb, acc, got,
    load_sem, theta_send, theta_recv, row_send, row_recv, keep_send, keep_recv,
    a_send, across_send, via_send, via_recv, far_send, a_recv, b_send, b_recv, rel_send, rel_recv, emf_send, emf_recv,
):
    phi, theta, row = lax.axis_index("phi"), lax.axis_index("theta"), lax.axis_index("row")
    group = theta % 2
    heavy_at, helper_at, far_at, light_at = 7 * group, 2 + 3 * group, 4 - group, 6 - 5 * group
    heavy, helper, far, light = theta == heavy_at, theta == helper_at, theta == far_at, theta == light_at
    source = heavy | light
    light_octet = 2 - 2 * group
    octet = jnp.where(light, light_octet, 0)
    my_i, my_half = phi // 2, phi % 2
    edge_i, main_i = 3 - 3 * row, row
    late = jnp.where(my_i == edge_i, ELAG, 0)

    def others(k):
        return lax.rem(phi + k, PHI)

    loads = [
        pltpu.make_async_copy(tf, xp.at[:, :, pl.ds(8, 32), :], load_sem.at[0]),
        pltpu.make_async_copy(vel, v, load_sem.at[1]),
        pltpu.make_async_copy(tab_hbm.at[theta], tab, load_sem.at[2]),
        pltpu.make_async_copy(fwd_hbm, fwd, load_sem.at[3]),
        pltpu.make_async_copy(inv_hbm, inv, load_sem.at[4]),
        pltpu.make_async_copy(one_hbm, one, load_sem.at[5]),
        pltpu.make_async_copy(back_hbm, back, load_sem.at[6]),
        pltpu.make_async_copy(modes_hbm, modes, load_sem.at[7]),
        pltpu.make_async_copy(tab_hbm.at[jnp.where(far, light_at, theta), 4], mask, load_sem.at[8]),
        pltpu.make_async_copy(kept_hbm, kept, load_sem.at[9]),
    ]
    for load in loads:
        load.start()

    barrier = pltpu.get_barrier_semaphore()
    pl.semaphore_signal(barrier, inc=1, device_id={"row": 1 - row}, device_id_type=MESH)
    for k in range(1, PHI):
        pl.semaphore_signal(barrier, inc=1, device_id={"phi": others(k)}, device_id_type=MESH)

    @pl.when(theta > 0)
    def _():
        pl.semaphore_signal(barrier, inc=1, device_id={"theta": theta - 1}, device_id_type=MESH)

    @pl.when(theta < 7)
    def _():
        pl.semaphore_signal(barrier, inc=1, device_id={"theta": theta + 1}, device_id_type=MESH)

    def greet_all(there):
        for k in range(PHI):
            pl.semaphore_signal(barrier, inc=1, device_id={"theta": there, "phi": others(k)}, device_id_type=MESH)

    def greet(there):
        pl.semaphore_signal(barrier, inc=1, device_id={"theta": there}, device_id_type=MESH)

    @pl.when(heavy)
    def _():
        greet_all(helper_at)
        greet(far_at)
        greet(light_at)

    @pl.when(helper)
    def _():
        greet_all(heavy_at)

    @pl.when(far)
    def _():
        greet_all(light_at)
        greet(heavy_at)

    @pl.when(light)
    def _():
        greet_all(far_at)
        greet(heavy_at)

    loads[0].wait()

    def pack(f, _):
        for i in range(4):
            edge[0, f, pl.ds(i, 1), :] = xp[f, i, pl.ds(8, 1), :]
            edge[1, f, pl.ds(i, 1), :] = xp[f, i, pl.ds(39, 1), :]
        return 0

    lax.fori_loop(0, 27, pack, 0)
    loads[9].wait()
    eye = lax.broadcasted_iota(jnp.int32, (32, 32), 0) == lax.broadcasted_iota(jnp.int32, (32, 32), 1)
    counts = jnp.where(eye, jnp.broadcast_to(kept[...], (32, 32)), 0).astype(F32)
    keep[0] = jnp.broadcast_to(jnp.sum(counts, axis=1, keepdims=True), (32, 128))

    peers = PHI + jnp.where(theta > 0, 1, 0) + jnp.where(theta < 7, 1, 0) + PHI
    peers = peers + jnp.where(heavy, 2, 0) + jnp.where(far | light, 1, 0)
    pl.semaphore_wait(barrier, peers)

    def theta_copy(n, side, there):
        first, last = PIECES[n]
        part = pl.ds(3 * first, 3 * (last - first))
        return pltpu.make_async_remote_copy(
            src_ref=edge.at[side, part], dst_ref=halo_t.at[side, part], send_sem=theta_send.at[side, n],
            recv_sem=theta_recv.at[side, n], device_id={"theta": there}, device_id_type=MESH)


    def row_copy(n):
        return pltpu.make_async_remote_copy(
            src_ref=xp.at[pl.ds(3 * n, 3), edge_i, pl.ds(8, 32), :], dst_ref=halo_r.at[pl.ds(3 * n, 3)],
            send_sem=row_send.at[n], recv_sem=row_recv.at[n],
            device_id={"row": 1 - row}, device_id_type=MESH)

    def send_theta(n):
        @pl.when(theta > 0)
        def _():
            theta_copy(n, 0, theta - 1).start()

        @pl.when(theta < 7)
        def _():
            theta_copy(n, 1, theta + 1).start()

    def wait_theta(n):
        @pl.when(theta > 0)
        def _():
            theta_copy(n, 0, theta).wait_send()
            theta_copy(n, 1, theta).wait_recv()

        @pl.when(theta < 7)
        def _():
            theta_copy(n, 1, theta).wait_send()
            theta_copy(n, 0, theta).wait_recv()

    send_theta(0)
    row_copy(0).start()
    send_theta(1)
    for n in range(1, AHEAD):
        row_copy(n).start()

    def keep_copy(slot, sem, there):
        return pltpu.make_async_remote_copy(
            src_ref=keep.at[0], dst_ref=keep.at[slot], send_sem=keep_send.at[sem], recv_sem=keep_recv.at[slot - 1],
            device_id={"theta": there}, device_id_type=MESH)

    @pl.when(heavy)
    def _():
        keep_copy(1, 0, helper_at).start()
        keep_copy(1, 1, far_at).start()

    @pl.when(light)
    def _():
        keep_copy(2, 0, far_at).start()

    for load in loads[1:9]:
        load.wait()
    outward, inward, metric = radial_constants()

    def radial(values, i):
        return jnp.where(row == 0, F32(values[i]), F32(values[i + 4]))

    for i in range(4):
        radius[0, i] = 0.2 * radial(outward, i) * (1.0 if i < 3 else jnp.where(row == 0, F32(1.0), F32(0.0)))
        radius[1, i] = 0.2 * radial(inward, i) * (1.0 if i > 0 else jnp.where(row == 1, F32(1.0), F32(0.0)))

    south, north = tab[0], tab[1]
    for i in range(4):
        g = 0.1 * radial(metric, i)
        cs, cn = g * south, g * north
        both = 0.2 * (radial(outward, i) + radial(inward, i))
        centre = (1.0 - both) - (cs + cn)
        for lanes in range(2):
            part = pl.ds(128 * lanes, 128)
            coef[0, i, :, part] = cs
            coef[1, i, :, part] = cn
            coef[2, i, :, part] = centre

    @pl.when(theta == 7)
    def _():
        halo_t[0] = jnp.zeros((27, 4, 256), F32)

    @pl.when(theta == 0)
    def _():
        halo_t[1] = jnp.zeros((27, 4, 256), F32)

    def drain(ref, sem):
        pltpu.make_async_copy(ref, ref, sem).wait()

    def chunk(n, p, rows):
        return st.at[pl.ds(3 * n, 3), p // 2, pl.ds(pl.multiple_of((rows + p % 2) * 8, 8), 8), :]

    def a_copy(n, p, there, rows, slot, sem):
        return pltpu.make_async_remote_copy(
            src_ref=chunk(n, p, rows), dst_ref=rx.at[slot, phi], send_sem=sem, recv_sem=a_recv.at[slot],
            device_id={"theta": there, "phi": p}, device_id_type=MESH)

    main_workers = [2 * main_i + lax.rem(phi + q, 6) for q in range(6)]
    edge_workers = [2 * edge_i + lax.rem(phi + q, 2) for q in range(2)]

    def far_octet(n):
        return jnp.where(member(n, OWN), 2, 0)

    def via_copy(n, part):
        r = rank(n, FARRED)
        layers = pl.ds(main_i, 3) if part == 0 else pl.ds(edge_i, 1)
        return pltpu.make_async_remote_copy(
            src_ref=st.at[pl.ds(3 * n, 3), layers, pl.ds(pl.multiple_of(far_octet(n) * 8, 8), 16), :],
            dst_ref=vb.at[r, :, layers], send_sem=via_send.at[part, lax.rem(r, ACROSS)],
            recv_sem=via_recv.at[part, r], device_id={"theta": light_at}, device_id_type=MESH)

    def pass_on(r, part):
        got_part = vb.at[r, :, pl.ds(main_i, 3)] if part == 0 else vb.at[r, :, pl.ds(edge_i, 1)]
        pltpu.make_async_copy(got_part, got_part, via_recv.at[part, r]).wait()
        slot = pick(r, [k for k, (kind, _) in enumerate(FAR_WORK) if kind == "H"])
        for p in main_workers if part == 0 else edge_workers:
            pltpu.make_async_remote_copy(
                src_ref=vb.at[r, :, p // 2, pl.ds(pl.multiple_of(p % 2 * 8, 8), 8), :],
                dst_ref=rx.at[slot, phi], send_sem=far_send, recv_sem=a_recv.at[slot],
                device_id={"theta": far_at, "phi": p}, device_id_type=MESH,
            ).start()

    def layer(n, i, neighbours):
        p_unit, q_unit = n // 3, n % 3
        unit = [jnp.where(p_unit == k, F32(0.5), F32(0.0)) for k in range(3)]
        weight = [jnp.where(q_unit == k, F32(1.0), F32(0.0)) for k in range(3)]
        profile = weight[0] + weight[1] * tab[2] + weight[2] * tab[3]
        profile = jnp.concatenate([profile, profile], axis=1)
        v0, v1, v2 = v[0, i], v[1, i], v[2, i]
        turned = (v1 * unit[2] - v2 * unit[1], v2 * unit[0] - v0 * unit[2], v0 * unit[1] - v1 * unit[0])
        for c in range(3):
            f = 3 * n + c
            xp[f, i, pl.ds(7, 1), :] = halo_t[1, f, pl.ds(i, 1), :]
            xp[f, i, pl.ds(40, 1), :] = halo_t[0, f, pl.ds(i, 1), :]
            total = coef[2, i] * xp[f, i, pl.ds(8, 32), :] + profile * turned[c]
            for factor, other in neighbours(f):
                total = total + factor * other
            total = total + coef[0, i] * xp[f, i, pl.ds(9, 32), :] + coef[1, i] * xp[f, i, pl.ds(7, 32), :]
            st[f, i] = total

        @pl.when(light)
        def _():
            rest = pl.ds(pl.multiple_of(16 - 8 * light_octet, 8), 16)
            for c in range(3):
                res[3 * n + c, i, rest, :] = st[3 * n + c, i, rest, :]

        @pl.when(jnp.logical_not(source))
        def _():
            for c in range(3):
                res[3 * n + c, i] = st[3 * n + c, i]

    def send(n, part):
        workers = main_workers if part == 0 else edge_workers

        @pl.when((heavy & member(n, OWN)) | (light & member(n, LIGHT_OWN)))
        def _():
            for p in workers:

                @pl.when(p == phi)
                def _(p=p):
                    pltpu.make_async_copy(chunk(n, p, octet), rx.at[n, phi], a_recv.at[n]).start()

                @pl.when(p != phi)
                def _(p=p):
                    a_copy(n, p, theta, octet, n, a_send).start()

        @pl.when(heavy & (n == DOUBLE))
        def _():
            for p in workers:

                @pl.when(p == phi)
                def _(p=p):
                    pltpu.make_async_copy(chunk(n, p, 2), rx.at[SECOND, phi], a_recv.at[SECOND]).start()

                @pl.when(p != phi)
                def _(p=p):
                    a_copy(n, p, theta, 2, SECOND, a_send).start()

        @pl.when(light & member(n, LIGHT_FAR))
        def _():
            slot = pick(rank(n, LIGHT_FAR), [k for k, (kind, _) in enumerate(FAR_WORK) if kind == "L"])
            for p in workers:
                a_copy(n, p, far_at, octet, slot, far_send).start()

        @pl.when(heavy & member(n, FARRED))
        def _():
            @pl.when(rank(n, FARRED) >= ACROSS)
            def _():
                via_copy(n, part).wait_send()

            via_copy(n, part).start()

        @pl.when(heavy & member(n, HELPED))
        def _():
            r = rank(n, HELPED)
            sem = across_send.at[part, lax.rem(r, ACROSS)]

            @pl.when(r >= ACROSS)
            def _():
                drain(rx.at[0, pl.ds(0, len(workers))], sem)

            for p in workers:
                a_copy(n, p, helper_at, 2, n, sem).start()

    def step_main(n):
        for k, (first, _) in enumerate(PIECES):

            @pl.when(n == first)
            def _(k=k):
                wait_theta(k)

        for k in range(2, len(PIECES)):

            @pl.when(n == PIECES[k][0] - 3)
            def _(k=k):
                send_theta(k)

        for m in range(3):
            i = main_i + m

            def neighbours(f, i=i):
                up, down = jnp.minimum(i + 1, 3), jnp.maximum(i - 1, 0)
                return (
                    (radius[0, i], xp[f, up, pl.ds(8, 32), :]),
                    (radius[1, i], xp[f, down, pl.ds(8, 32), :]),
                )

            layer(n, i, neighbours)
        send(n, 0)

    def step_edge(n):
        row_copy(n).wait_recv()
        row_copy(n).wait_send()

        @pl.when(n + AHEAD < STAGES)
        def _():
            row_copy(n + AHEAD).start()

        def neighbours(f):
            return (
                (radius[row, edge_i], halo_r[f]),
                (radius[1 - row, edge_i], xp[f, 2 - row, pl.ds(8, 32), :]),
            )

        layer(n, edge_i, neighbours)
        send(n, 1)

    half_rows = pl.ds(pl.multiple_of(my_half * 8, 8), 8)

    def gather_copy(slot, p):
        return pltpu.make_async_remote_copy(
            src_ref=yb.at[slot, p], dst_ref=rel.at[slot, :, my_i, half_rows, :],
            send_sem=b_send, recv_sem=rel_recv.at[slot], device_id={"phi": p}, device_id_type=MESH)

    far_light = [1 if kind == "L" else 0 for kind, _ in FAR_WORK]
    far_stage = [n for _, n in FAR_WORK]

    def relay(slot):
        pltpu.make_async_copy(rel.at[slot], rel.at[slot], rel_recv.at[slot]).wait()
        to_light = far & (pick(slot, far_light) == 1)
        n = jnp.where(far, pick(slot, far_stage), slot)
        rows = jnp.where(to_light, light_octet, jnp.where(far, far_octet(n), 2))
        pltpu.make_async_remote_copy(
            src_ref=rel.at[slot],
            dst_ref=res.at[pl.ds(3 * n, 3), :, pl.ds(pl.multiple_of(rows * 8, 8), 16), :],
            send_sem=rel_send, recv_sem=b_recv.at[n],
            device_id={"theta": jnp.where(to_light, light_at, heavy_at)}, device_id_type=MESH,
        ).start()

    def work(slot):
        @pl.when((helper & (slot == HELPED[0])) | (far & (slot == 0)))
        def _():
            keep_copy(1, 0, theta).wait_recv()

        @pl.when(far & (slot == 0))
        def _():
            keep_copy(2, 0, theta).wait_recv()

        on_light = far & (pick(slot, far_light) == 1)
        far_rows = jnp.where(on_light, light_octet, far_octet(pick(slot, far_stage)))
        rows = jnp.where(far, far_rows, jnp.where(helper | (slot == SECOND), 2, octet)) + my_half
        mine = pl.ds(pl.multiple_of(rows * 8, 8), 8)
        kept_rows = keep[jnp.where(on_light, 2, jnp.where(source, 0, 1)), mine, :]
        kept_rows = jnp.concatenate([kept_rows, kept_rows], axis=1)
        polar = jnp.maximum(mask[mine, :], jnp.where(light | on_light, F32(0.0), F32(1.0)))
        polar = jnp.concatenate([polar, polar], axis=1) > 0.5
        pltpu.make_async_copy(rx.at[slot], rx.at[slot], a_recv.at[slot]).wait()
        blocks = [rx[slot, p].reshape(24, 256) for p in range(PHI)]
        done = filter_lines(blocks, kept_rows, modes, fwd, inv, one, back)
        for p in range(PHI):
            yb[slot, p] = jnp.where(polar[None], done[p].reshape(3, 8, 256), rx[slot, p])

        @pl.when(source)
        def _():
            n = jnp.where(slot == SECOND, DOUBLE, slot)
            here = res.at[pl.ds(3 * n, 3), my_i, mine, :]
            pltpu.make_async_copy(yb.at[slot, phi], here, b_recv.at[n]).start()
            for k in range(1, PHI):
                pltpu.make_async_remote_copy(
                    src_ref=yb.at[slot, others(k)], dst_ref=here, send_sem=b_send, recv_sem=b_recv.at[n],
                    device_id={"phi": others(k)}, device_id_type=MESH,
                ).start()

        @pl.when(jnp.logical_not(source))
        def _():
            pltpu.make_async_copy(
                yb.at[slot, phi], rel.at[slot, :, my_i, half_rows, :], rel_recv.at[slot]
            ).start()
            for k in range(1, PHI):
                gather_copy(slot, others(k)).start()

    acc[...] = jnp.zeros((32, 128), F32)
    lane = lax.broadcasted_iota(jnp.int32, (32, 128), 1)

    def finish(n):
        @pl.when(heavy)
        def _():
            whole = res.at[pl.ds(3 * n, 3)]
            pltpu.make_async_copy(whole, whole, b_recv.at[n]).wait()

        @pl.when(light)
        def _():
            part = res.at[pl.ds(3 * n, 3), :, pl.ds(pl.multiple_of(octet * 8, 8), 16), :]
            pltpu.make_async_copy(part, part, b_recv.at[n]).wait()

        total = acc[...]
        for i in range(4):
            v0, v1, v2 = v[0, i], v[1, i], v[2, i]
            r0, r1, r2 = res[3 * n, i], res[3 * n + 1, i], res[3 * n + 2, i]
            terms = (v1 * r2 - v2 * r1, v2 * r0 - v0 * r2, v0 * r1 - v1 * r0)
            for c in range(3):
                summed = jnp.sum(terms[c][:, :128] + terms[c][:, 128:], axis=1, keepdims=True)
                total = jnp.where(lane == 27 * i + 3 * n + c, jnp.broadcast_to(summed, (32, 128)), total)
        acc[...] = total

    def tick(t, _):
        @pl.when(t < STAGES)
        def _():
            step_main(t)

        @pl.when((t >= ELAG) & (t < STAGES + ELAG))
        def _():
            step_edge(t - ELAG)

        for part in range(2):
            first = VIA + ELAG * part

            @pl.when(light & (t >= first) & (t < first + len(FARRED)))
            def _(part=part, first=first):
                pass_on(t - first, part)

        def busy(slot):
            mine = (heavy & member(slot, OWN)) | (light & member(slot, LIGHT_OWN))
            theirs = (helper & member(slot, HELPED)) | (far & (slot >= 0) & (slot < len(FAR_WORK)))
            return mine | theirs

        at = t - jnp.where(helper, HELP, jnp.where(far, FAR, jnp.where(light, LIGHT_BEHIND, BEHIND)))

        slot = at - late

        def work_on(m, _):
            work(jnp.where(m == 1, SECOND, slot))
            return 0

        halves = jnp.where(busy(slot), 1, 0) + jnp.where(heavy & (slot == DOUBLE), 1, 0)
        lax.fori_loop(0, halves, work_on, 0)

        @pl.when((helper | far) & busy(at - ELAG - 1))
        def _():
            relay(at - ELAG - 1)

        @pl.when(t >= LAG)
        def _():
            finish(t - LAG)

        return 0

    lax.fori_loop(0, STAGES + LAG, tick, 0)

    def emf_copy(k):
        p = others(k)
        return pltpu.make_async_remote_copy(
            src_ref=acc.at[pl.ds(pl.multiple_of(p // 2 * 8, 8), 8), :], dst_ref=got.at[phi],
            send_sem=emf_send, recv_sem=emf_recv, device_id={"phi": p}, device_id_type=MESH)

    for k in range(1, PHI):
        emf_copy(k).start()
    pltpu.make_async_copy(acc.at[pl.ds(pl.multiple_of(phi // 2 * 8, 8), 8), :], got.at[phi], emf_recv).start()
    pltpu.make_async_copy(got, got, emf_recv).wait()
    summed = got[0]
    for p in range(1, PHI):
        summed = summed + got[p]
    summed = summed * (1.0 / NPHI)
    mean = jnp.where(phi % 2 == 0, summed[:4], summed[4:])
    for i in range(4):
        emf[i] = mean[:, 27 * i : 27 * i + 27]

    seven = got.at[pl.ds(0, 7)]
    drain(seven, emf_send)

    @pl.when(heavy)
    def _():
        keep_copy(1, 0, theta).wait_send()
        keep_copy(1, 1, theta).wait_send()
        for n in range(ACROSS):
            drain(rx.at[0, pl.ds(0, 6)], across_send.at[0, n])
            drain(rx.at[0, pl.ds(0, 2)], across_send.at[1, n])
            drain(vb.at[0, :, pl.ds(0, 3)], via_send.at[0, n])
            drain(vb.at[0, :, pl.ds(0, 1)], via_send.at[1, n])
        drain(rx.at[pl.ds(0, len(OWN) + 1), pl.ds(0, 7)], a_send)
        drain(yb.at[pl.ds(0, len(OWN) + 1), pl.ds(0, 7)], b_send)

    @pl.when(light)
    def _():
        keep_copy(2, 0, theta).wait_send()
        drain(rx.at[pl.ds(0, len(LIGHT_OWN)), pl.ds(0, 7)], a_send)
        drain(yb.at[pl.ds(0, len(LIGHT_OWN)), pl.ds(0, 7)], b_send)
        drain(rx.at[pl.ds(0, len(FAR_WORK))], far_send)

    @pl.when(helper)
    def _():
        drain(yb.at[pl.ds(0, len(HELPED)), pl.ds(0, 7)], b_send)
        drain(rel.at[pl.ds(0, len(HELPED))], rel_send)

    @pl.when(far)
    def _():
        drain(yb.at[pl.ds(0, len(FAR_WORK)), pl.ds(0, 7)], b_send)
        drain(rel.at[pl.ds(0, len(FAR_WORK))], rel_send)


def body(test_fields, velocity, kept):
    forward, inverse, singles, singles_back, modes = fourier_constants()
    tables = row_tables()
    hbm, vmem = pl.BlockSpec(memory_space=pltpu.HBM), pl.BlockSpec(memory_space=pltpu.VMEM)
    dma = pltpu.SemaphoreType.DMA
    result, emf = pl.pallas_call(
        kernel,
        out_shape=(
            jax.ShapeDtypeStruct((27, 4, 32, 256), F32),
            jax.ShapeDtypeStruct((4, 4, 27), F32),
        ),
        in_specs=[hbm] * 9,
        out_specs=(vmem, vmem),
        scratch_shapes=[
            pltpu.VMEM((27, 4, 48, 256), F32),
            pltpu.VMEM((3, 4, 32, 256), F32),
            pltpu.VMEM((1, 32), jnp.int32),
            pltpu.VMEM((5, 32, 128), F32),
            pltpu.VMEM(forward.shape, BF16),
            pltpu.VMEM(inverse.shape, BF16),
            pltpu.VMEM(singles.shape, BF16),
            pltpu.VMEM(singles_back.shape, BF16),
            pltpu.VMEM(modes.shape, F32),
            pltpu.VMEM((2, 27, 4, 256), F32),
            pltpu.VMEM((2, 27, 4, 256), F32),
            pltpu.VMEM((27, 32, 256), F32),
            pltpu.VMEM((3, 4, 32, 256), F32),
            pltpu.SMEM((2, 4), F32),
            pltpu.VMEM((3, 32, 128), F32),
            pltpu.VMEM((32, 128), F32),
            pltpu.VMEM((27, 4, 32, 256), F32),
            pltpu.VMEM((STAGES + 1, PHI, 3, 8, 256), F32),
            pltpu.VMEM((STAGES + 1, PHI, 3, 8, 256), F32),
            pltpu.VMEM((STAGES, 3, 4, 16, 256), F32),
            pltpu.VMEM((len(FARRED), 3, 4, 16, 256), F32),
            pltpu.VMEM((32, 128), F32),
            pltpu.VMEM((PHI, 8, 128), F32),
            dma((10,)),
            dma((2, len(PIECES))),
            dma((2, len(PIECES))),
            dma((STAGES,)),
            dma((STAGES,)),
            dma((2,)),
            dma((2,)),
            dma,
            dma((2, ACROSS)),
            dma((2, ACROSS)),
            dma((2, len(FARRED))),
            dma,
            dma((STAGES + 1,)),
            dma,
            dma((STAGES,)),
            dma,
            dma((STAGES,)),
            dma,
            dma,
        ],
        compiler_params=pltpu.CompilerParams(
            collective_id=0, has_side_effects=True, vmem_limit_bytes=40 * 2**20
        ),
        name="substep",
    )(
        *(
            pltpu.with_memory_space_constraint(jnp.asarray(a), pltpu.HBM)
            for a in (
                test_fields, velocity, kept.reshape(1, 32), tables, forward, inverse, singles, singles_back, modes,
            )
        )
    )
    return result, jnp.transpose(emf, (2, 0, 1))


def solution(mesh):
    return jax.shard_map(
        body,
        mesh=mesh,
        in_specs=(P(None, "row", "theta", "phi"), P(None, "row", "theta", "phi"), P("theta")),
        out_specs=(P(None, "row", "theta", "phi"), P(None, "row", ("theta", "phi"))),
        check_vma=False,
    )
```

```python
import functools
import math

import jax
import jax.numpy as jnp
import ml_dtypes
import numpy as np
from jax import lax
from jax.experimental import pallas as pl
from jax.experimental.pallas import tpu as pltpu
from jax.sharding import PartitionSpec as P

MESH = pl.DeviceIdType.MESH
NPHI = 2048
MMAX = 512
STAGES = 9
AHEAD = 3
ELAG = 1
PIECES = ((0, 1), (1, 3), (3, 5), (5, 7), (7, 9))
ACROSS = 2
LAG = 12
BEHIND = 4
LIGHT_BEHIND = 4
HELP = 0
FAR = 0
VIA = 2
PLAN = ("FH", "OF", "OH", "FH", "OF", "OH", "OH", "OO", "OH")
FAR_WORK = (("L", 0), ("H", 0), ("H", 1), ("H", 3), ("H", 4))
OWN = tuple(n for n in range(STAGES) if "O" in PLAN[n])
DOUBLE = PLAN.index("OO")
SECOND = STAGES
HELPED = tuple(n for n in range(STAGES) if "H" in PLAN[n])
FARRED = tuple(n for n in range(STAGES) if "F" in PLAN[n])
LIGHT_FAR = tuple(n for kind, n in FAR_WORK if kind == "L")
LIGHT_OWN = tuple(n for n in range(STAGES) if n not in LIGHT_FAR)
PHI = 8
F32 = jnp.float32
BF16 = jnp.bfloat16


def split_bf16(a):
    hi = a.astype(ml_dtypes.bfloat16)
    lo = (a - hi.astype(np.float64)).astype(ml_dtypes.bfloat16)
    return np.stack([hi, lo])


def fourier_constants():
    cell = np.arange(256)
    block = np.arange(64)

    def tables(mode):
        angle = 2.0 * math.pi * ((cell[:, None] * mode[None, :]) % NPHI) / NPHI
        return np.cos(angle), np.sin(angle)

    def scale(mode):
        return np.where(mode == 0, 1.0 / NPHI, 2.0 / NPHI)

    forward, inverse, modes = [], [], []
    singles, singles_back = [], []
    for r in (0, 4):
        mode = 8 * block + r
        c, s = tables(mode)
        full = np.concatenate([c, s], axis=1)
        singles.append(full)
        singles_back.append((full * np.tile(scale(mode), 2)).T)
        modes.append(np.tile(mode, 2))
    modes = [np.concatenate(modes)]
    for r in (1, 2, 3):
        m, n = 8 * block + r, 8 * block + 8 - r
        cm, sm = tables(m)
        cn, sn = tables(n)
        upper = np.concatenate([cm, sm, cn, sn], axis=1)
        lower = np.concatenate([-sm, cm, sn, -cn], axis=1)
        full = np.concatenate([upper, lower], axis=0)
        weights = np.concatenate([scale(m), scale(m), scale(n), scale(n)])
        forward.append(full)
        inverse.append((full * weights).T)
        modes.append(np.concatenate([m, m, n, n]))
    modes = np.broadcast_to(np.stack(modes).astype(np.float32)[:, None, :], (4, 8, 256))
    return (
        split_bf16(np.stack(forward)),
        split_bf16(np.stack(inverse)),
        split_bf16(np.stack(singles)),
        split_bf16(np.stack(singles_back)),
        np.ascontiguousarray(modes),
    )


def row_tables():
    j = np.arange(256)
    d = math.pi / 256
    angle = d * (j + 0.5)
    south = np.sin(angle + 0.5 * d) / np.sin(angle)
    north = np.sin(angle - 0.5 * d) / np.sin(angle)
    polar = (3 * (2 * j + 1) < 256) | (3 * (2 * (255 - j) + 1) < 256)
    kinds = np.stack([south, north, np.cos(angle), np.sin(angle), polar.astype(np.float64)])
    kinds = kinds.reshape(5, 8, 32).transpose(1, 0, 2)
    return np.ascontiguousarray(np.broadcast_to(kinds[..., None], (8, 5, 32, 128)).astype(np.float32))


def radial_constants():
    h = 0.3 / 8
    r = 0.7 + h * (np.arange(8) + 0.5)
    return ((r + h / 2) / r) ** 2, ((r - h / 2) / r) ** 2, (1.0 / r) ** 2


def split_rows(a):
    hi = a.astype(BF16).astype(F32)
    return jnp.concatenate([hi, a - hi], axis=0).astype(BF16)


def dot(a, b):
    return jnp.dot(a, b, preferred_element_type=F32)


def dot_split(a, high, low):
    lines = a.shape[0]
    both = split_rows(a)
    out = dot(both, high) + dot(both, low)
    return out[:lines] + out[lines:]


def filter_lines(blocks, keep, modes, fwd, inv, one, back):
    x0, x1, x2, x3, x4, x5, x6, x7 = blocks
    half = math.sqrt(0.5)
    s04, d04, s26, d26 = x0 + x4, x0 - x4, x2 + x6, x2 - x6
    s15, d15, s37, d37 = x1 + x5, x1 - x5, x3 + x7, x3 - x7
    even, odd = s04 + s26, s15 + s37
    cross, plus = half * (d15 - d37), half * (d15 + d37)
    pairs = [(d04 + cross, d26 + plus), (s04 - s26, s15 - s37), (d04 - cross, plus - d26)]

    def masked(mid, group):
        lines = mid.shape[0]
        kept = mid.reshape(lines // 8, 8, 256)
        kept = jnp.where((modes[group] < keep)[None], kept, 0.0)
        return kept.reshape(lines, 256)

    mid = jnp.concatenate(
        [dot_split(even + odd, one[0, 0], one[1, 0]), dot_split(even - odd, one[0, 1], one[1, 1])], axis=1
    )
    mid = masked(mid, 0)
    p0 = dot_split(mid[:, :128], back[0, 0], back[1, 0])
    p4 = dot_split(mid[:, 128:], back[0, 1], back[1, 1])
    p, q = [], []
    for r, (u, v) in enumerate(pairs):
        mid = dot_split(jnp.concatenate([u, v], axis=1), fwd[0, r], fwd[1, r])
        mid = masked(mid, r + 1)
        out = dot_split(mid, inv[0, r], inv[1, r])
        p.append(out[:, :256])
        q.append(out[:, 256:])
    (p1, p2, p3), (q1, q2, q3) = p, q
    a, b = p0 + p4, p0 - p4
    p13, q13 = p1 + p3, q1 - q3
    ph, qh = half * (p1 - p3), half * (q1 + q3)
    ap, am, bp, bm = a + p2, a - p2, b + q2, b - q2
    return [
        ap + p13,
        bp + (ph + qh),
        am + q13,
        bm - (ph - qh),
        ap - p13,
        bp - (ph + qh),
        am - q13,
        bm + (ph - qh),
    ]


def member(n, values):
    found = n == values[0]
    for value in values[1:]:
        found = found | (n == value)
    return found


def rank(n, values):
    return sum(jnp.where(n > value, 1, 0) for value in values)


def pick(n, values):
    out = values[0]
    for k in range(1, len(values)):
        out = jnp.where(n >= k, values[k], out)
    return out


def kernel(
    tf, vel, kept_hbm, tab_hbm, fwd_hbm, inv_hbm, one_hbm, back_hbm, modes_hbm,
    res, emf,
    xp, v, kept, tab, fwd, inv, one, back, modes,
    edge, halo_t, halo_r, coef, radius, keep, mask, st, rx, yb, rel, vb, acc, got,
    load_sem, theta_send, theta_recv, row_send, row_recv, keep_send, keep_recv,
    a_send, across_send, via_send, via_recv, far_send, a_recv, b_send, b_recv, rel_send, rel_recv, emf_send, emf_recv,
):
    phi, theta, row = lax.axis_index("phi"), lax.axis_index("theta"), lax.axis_index("row")
    group = theta % 2
    heavy_at, helper_at, far_at, light_at = 7 * group, 2 + 3 * group, 4 - group, 6 - 5 * group
    heavy, helper, far, light = theta == heavy_at, theta == helper_at, theta == far_at, theta == light_at
    source = heavy | light
    light_octet = 2 - 2 * group
    octet = jnp.where(light, light_octet, 0)
    my_i, my_half = phi // 2, phi % 2
    edge_i, main_i = 3 - 3 * row, row
    late = jnp.where(my_i == edge_i, ELAG, 0)

    def others(k):
        return lax.rem(phi + k, PHI)

    loads = [
        pltpu.make_async_copy(tf, xp.at[:, :, pl.ds(8, 32), :], load_sem.at[0]),
        pltpu.make_async_copy(vel, v, load_sem.at[1]),
        pltpu.make_async_copy(tab_hbm.at[theta], tab, load_sem.at[2]),
        pltpu.make_async_copy(fwd_hbm, fwd, load_sem.at[3]),
        pltpu.make_async_copy(inv_hbm, inv, load_sem.at[4]),
        pltpu.make_async_copy(one_hbm, one, load_sem.at[5]),
        pltpu.make_async_copy(back_hbm, back, load_sem.at[6]),
        pltpu.make_async_copy(modes_hbm, modes, load_sem.at[7]),
        pltpu.make_async_copy(tab_hbm.at[jnp.where(far, light_at, theta), 4], mask, load_sem.at[8]),
        pltpu.make_async_copy(kept_hbm, kept, load_sem.at[9]),
    ]
    for load in loads:
        load.start()

    barrier = pltpu.get_barrier_semaphore()
    pl.semaphore_signal(barrier, inc=1, device_id={"row": 1 - row}, device_id_type=MESH)
    for k in range(1, PHI):
        pl.semaphore_signal(barrier, inc=1, device_id={"phi": others(k)}, device_id_type=MESH)

    @pl.when(theta > 0)
    def _():
        pl.semaphore_signal(barrier, inc=1, device_id={"theta": theta - 1}, device_id_type=MESH)

    @pl.when(theta < 7)
    def _():
        pl.semaphore_signal(barrier, inc=1, device_id={"theta": theta + 1}, device_id_type=MESH)

    def greet_all(there):
        for k in range(PHI):
            pl.semaphore_signal(barrier, inc=1, device_id={"theta": there, "phi": others(k)}, device_id_type=MESH)

    def greet(there):
        pl.semaphore_signal(barrier, inc=1, device_id={"theta": there}, device_id_type=MESH)

    @pl.when(heavy)
    def _():
        greet_all(helper_at)
        greet(far_at)
        greet(light_at)

    @pl.when(helper)
    def _():
        greet_all(heavy_at)

    @pl.when(far)
    def _():
        greet_all(light_at)
        greet(heavy_at)

    @pl.when(light)
    def _():
        greet_all(far_at)
        greet(heavy_at)

    loads[0].wait()

    def pack(f, _):
        for i in range(4):
            edge[0, f, pl.ds(i, 1), :] = xp[f, i, pl.ds(8, 1), :]
            edge[1, f, pl.ds(i, 1), :] = xp[f, i, pl.ds(39, 1), :]
        return 0

    lax.fori_loop(0, 27, pack, 0)
    loads[9].wait()
    eye = lax.broadcasted_iota(jnp.int32, (32, 32), 0) == lax.broadcasted_iota(jnp.int32, (32, 32), 1)
    counts = jnp.where(eye, jnp.broadcast_to(kept[...], (32, 32)), 0).astype(F32)
    keep[0] = jnp.broadcast_to(jnp.sum(counts, axis=1, keepdims=True), (32, 128))

    peers = PHI + jnp.where(theta > 0, 1, 0) + jnp.where(theta < 7, 1, 0) + PHI
    peers = peers + jnp.where(heavy, 2, 0) + jnp.where(far | light, 1, 0)
    pl.semaphore_wait(barrier, peers)

    def theta_copy(n, side, there):
        first, last = PIECES[n]
        part = pl.ds(3 * first, 3 * (last - first))
        return pltpu.make_async_remote_copy(
            src_ref=edge.at[side, part], dst_ref=halo_t.at[side, part], send_sem=theta_send.at[side, n],
            recv_sem=theta_recv.at[side, n], device_id={"theta": there}, device_id_type=MESH)


    def row_copy(n):
        return pltpu.make_async_remote_copy(
            src_ref=xp.at[pl.ds(3 * n, 3), edge_i, pl.ds(8, 32), :], dst_ref=halo_r.at[pl.ds(3 * n, 3)],
            send_sem=row_send.at[n], recv_sem=row_recv.at[n],
            device_id={"row": 1 - row}, device_id_type=MESH)

    def send_theta(n):
        @pl.when(theta > 0)
        def _():
            theta_copy(n, 0, theta - 1).start()

        @pl.when(theta < 7)
        def _():
            theta_copy(n, 1, theta + 1).start()

    def wait_theta(n):
        @pl.when(theta > 0)
        def _():
            theta_copy(n, 0, theta).wait_send()
            theta_copy(n, 1, theta).wait_recv()

        @pl.when(theta < 7)
        def _():
            theta_copy(n, 1, theta).wait_send()
            theta_copy(n, 0, theta).wait_recv()

    send_theta(0)
    row_copy(0).start()
    send_theta(1)
    for n in range(1, AHEAD):
        row_copy(n).start()

    def keep_copy(slot, sem, there):
        return pltpu.make_async_remote_copy(
            src_ref=keep.at[0], dst_ref=keep.at[slot], send_sem=keep_send.at[sem], recv_sem=keep_recv.at[slot - 1],
            device_id={"theta": there}, device_id_type=MESH)

    @pl.when(heavy)
    def _():
        keep_copy(1, 0, helper_at).start()
        keep_copy(1, 1, far_at).start()

    @pl.when(light)
    def _():
        keep_copy(2, 0, far_at).start()

    for load in loads[1:9]:
        load.wait()
    outward, inward, metric = radial_constants()

    def radial(values, i):
        return jnp.where(row == 0, F32(values[i]), F32(values[i + 4]))

    for i in range(4):
        radius[0, i] = 0.2 * radial(outward, i) * (1.0 if i < 3 else jnp.where(row == 0, F32(1.0), F32(0.0)))
        radius[1, i] = 0.2 * radial(inward, i) * (1.0 if i > 0 else jnp.where(row == 1, F32(1.0), F32(0.0)))

    south, north = tab[0], tab[1]
    for i in range(4):
        g = 0.1 * radial(metric, i)
        cs, cn = g * south, g * north
        both = 0.2 * (radial(outward, i) + radial(inward, i))
        centre = (1.0 - both) - (cs + cn)
        for lanes in range(2):
            part = pl.ds(128 * lanes, 128)
            coef[0, i, :, part] = cs
            coef[1, i, :, part] = cn
            coef[2, i, :, part] = centre

    @pl.when(theta == 7)
    def _():
        halo_t[0] = jnp.zeros((27, 4, 256), F32)

    @pl.when(theta == 0)
    def _():
        halo_t[1] = jnp.zeros((27, 4, 256), F32)

    def drain(ref, sem):
        pltpu.make_async_copy(ref, ref, sem).wait()

    def chunk(n, p, rows):
        return st.at[pl.ds(3 * n, 3), p // 2, pl.ds(pl.multiple_of((rows + p % 2) * 8, 8), 8), :]

    def a_copy(n, p, there, rows, slot, sem):
        return pltpu.make_async_remote_copy(
            src_ref=chunk(n, p, rows), dst_ref=rx.at[slot, phi], send_sem=sem, recv_sem=a_recv.at[slot],
            device_id={"theta": there, "phi": p}, device_id_type=MESH)

    main_workers = [2 * main_i + lax.rem(phi + q, 6) for q in range(6)]
    edge_workers = [2 * edge_i + lax.rem(phi + q, 2) for q in range(2)]

    def far_octet(n):
        return jnp.where(member(n, OWN), 2, 0)

    def via_copy(n, part):
        r = rank(n, FARRED)
        layers = pl.ds(main_i, 3) if part == 0 else pl.ds(edge_i, 1)
        return pltpu.make_async_remote_copy(
            src_ref=st.at[pl.ds(3 * n, 3), layers, pl.ds(pl.multiple_of(far_octet(n) * 8, 8), 16), :],
            dst_ref=vb.at[r, :, layers], send_sem=via_send.at[part, lax.rem(r, ACROSS)],
            recv_sem=via_recv.at[part, r], device_id={"theta": light_at}, device_id_type=MESH)

    def pass_on(r, part):
        got_part = vb.at[r, :, pl.ds(main_i, 3)] if part == 0 else vb.at[r, :, pl.ds(edge_i, 1)]
        pltpu.make_async_copy(got_part, got_part, via_recv.at[part, r]).wait()
        slot = pick(r, [k for k, (kind, _) in enumerate(FAR_WORK) if kind == "H"])
        for p in main_workers if part == 0 else edge_workers:
            pltpu.make_async_remote_copy(
                src_ref=vb.at[r, :, p // 2, pl.ds(pl.multiple_of(p % 2 * 8, 8), 8), :],
                dst_ref=rx.at[slot, phi], send_sem=far_send, recv_sem=a_recv.at[slot],
                device_id={"theta": far_at, "phi": p}, device_id_type=MESH,
            ).start()

    def layer(n, i, neighbours):
        p_unit, q_unit = n // 3, n % 3
        unit = [jnp.where(p_unit == k, F32(0.5), F32(0.0)) for k in range(3)]
        weight = [jnp.where(q_unit == k, F32(1.0), F32(0.0)) for k in range(3)]
        profile = weight[0] + weight[1] * tab[2] + weight[2] * tab[3]
        profile = jnp.concatenate([profile, profile], axis=1)
        v0, v1, v2 = v[0, i], v[1, i], v[2, i]
        turned = (v1 * unit[2] - v2 * unit[1], v2 * unit[0] - v0 * unit[2], v0 * unit[1] - v1 * unit[0])
        for c in range(3):
            f = 3 * n + c
            xp[f, i, pl.ds(7, 1), :] = halo_t[1, f, pl.ds(i, 1), :]
            xp[f, i, pl.ds(40, 1), :] = halo_t[0, f, pl.ds(i, 1), :]
            total = coef[2, i] * xp[f, i, pl.ds(8, 32), :] + profile * turned[c]
            for factor, other in neighbours(f):
                total = total + factor * other
            total = total + coef[0, i] * xp[f, i, pl.ds(9, 32), :] + coef[1, i] * xp[f, i, pl.ds(7, 32), :]
            st[f, i] = total

        @pl.when(light)
        def _():
            rest = pl.ds(pl.multiple_of(16 - 8 * light_octet, 8), 16)
            for c in range(3):
                res[3 * n + c, i, rest, :] = st[3 * n + c, i, rest, :]

        @pl.when(jnp.logical_not(source))
        def _():
            for c in range(3):
                res[3 * n + c, i] = st[3 * n + c, i]

    def send(n, part):
        workers = main_workers if part == 0 else edge_workers

        @pl.when((heavy & member(n, OWN)) | (light & member(n, LIGHT_OWN)))
        def _():
            for p in workers:

                @pl.when(p == phi)
                def _(p=p):
                    pltpu.make_async_copy(chunk(n, p, octet), rx.at[n, phi], a_recv.at[n]).start()

                @pl.when(p != phi)
                def _(p=p):
                    a_copy(n, p, theta, octet, n, a_send).start()

        @pl.when(heavy & (n == DOUBLE))
        def _():
            for p in workers:

                @pl.when(p == phi)
                def _(p=p):
                    pltpu.make_async_copy(chunk(n, p, 2), rx.at[SECOND, phi], a_recv.at[SECOND]).start()

                @pl.when(p != phi)
                def _(p=p):
                    a_copy(n, p, theta, 2, SECOND, a_send).start()

        @pl.when(light & member(n, LIGHT_FAR))
        def _():
            slot = pick(rank(n, LIGHT_FAR), [k for k, (kind, _) in enumerate(FAR_WORK) if kind == "L"])
            for p in workers:
                a_copy(n, p, far_at, octet, slot, far_send).start()

        @pl.when(heavy & member(n, FARRED))
        def _():
            @pl.when(rank(n, FARRED) >= ACROSS)
            def _():
                via_copy(n, part).wait_send()

            via_copy(n, part).start()

        @pl.when(heavy & member(n, HELPED))
        def _():
            r = rank(n, HELPED)
            sem = across_send.at[part, lax.rem(r, ACROSS)]

            @pl.when(r >= ACROSS)
            def _():
                drain(rx.at[0, pl.ds(0, len(workers))], sem)

            for p in workers:
                a_copy(n, p, helper_at, 2, n, sem).start()

    def step_main(n):
        for k, (first, _) in enumerate(PIECES):

            @pl.when(n == first)
            def _(k=k):
                wait_theta(k)

        for k in range(2, len(PIECES)):

            @pl.when(n == PIECES[k][0] - 3)
            def _(k=k):
                send_theta(k)

        for m in range(3):
            i = main_i + m

            def neighbours(f, i=i):
                up, down = jnp.minimum(i + 1, 3), jnp.maximum(i - 1, 0)
                return (
                    (radius[0, i], xp[f, up, pl.ds(8, 32), :]),
                    (radius[1, i], xp[f, down, pl.ds(8, 32), :]),
                )

            layer(n, i, neighbours)
        send(n, 0)

    def step_edge(n):
        row_copy(n).wait_recv()
        row_copy(n).wait_send()

        @pl.when(n + AHEAD < STAGES)
        def _():
            row_copy(n + AHEAD).start()

        def neighbours(f):
            return (
                (radius[row, edge_i], halo_r[f]),
                (radius[1 - row, edge_i], xp[f, 2 - row, pl.ds(8, 32), :]),
            )

        layer(n, edge_i, neighbours)
        send(n, 1)

    half_rows = pl.ds(pl.multiple_of(my_half * 8, 8), 8)

    def gather_copy(slot, p):
        return pltpu.make_async_remote_copy(
            src_ref=yb.at[slot, p], dst_ref=rel.at[slot, :, my_i, half_rows, :],
            send_sem=b_send, recv_sem=rel_recv.at[slot], device_id={"phi": p}, device_id_type=MESH)

    far_light = [1 if kind == "L" else 0 for kind, _ in FAR_WORK]
    far_stage = [n for _, n in FAR_WORK]

    def relay(slot):
        pltpu.make_async_copy(rel.at[slot], rel.at[slot], rel_recv.at[slot]).wait()
        to_light = far & (pick(slot, far_light) == 1)
        n = jnp.where(far, pick(slot, far_stage), slot)
        rows = jnp.where(to_light, light_octet, jnp.where(far, far_octet(n), 2))
        pltpu.make_async_remote_copy(
            src_ref=rel.at[slot],
            dst_ref=res.at[pl.ds(3 * n, 3), :, pl.ds(pl.multiple_of(rows * 8, 8), 16), :],
            send_sem=rel_send, recv_sem=b_recv.at[n],
            device_id={"theta": jnp.where(to_light, light_at, heavy_at)}, device_id_type=MESH,
        ).start()

    def work(slot):
        @pl.when((helper & (slot == HELPED[0])) | (far & (slot == 0)))
        def _():
            keep_copy(1, 0, theta).wait_recv()

        @pl.when(far & (slot == 0))
        def _():
            keep_copy(2, 0, theta).wait_recv()

        on_light = far & (pick(slot, far_light) == 1)
        far_rows = jnp.where(on_light, light_octet, far_octet(pick(slot, far_stage)))
        rows = jnp.where(far, far_rows, jnp.where(helper | (slot == SECOND), 2, octet)) + my_half
        mine = pl.ds(pl.multiple_of(rows * 8, 8), 8)
        kept_rows = keep[jnp.where(on_light, 2, jnp.where(source, 0, 1)), mine, :]
        kept_rows = jnp.concatenate([kept_rows, kept_rows], axis=1)
        polar = jnp.maximum(mask[mine, :], jnp.where(light | on_light, F32(0.0), F32(1.0)))
        polar = jnp.concatenate([polar, polar], axis=1) > 0.5
        pltpu.make_async_copy(rx.at[slot], rx.at[slot], a_recv.at[slot]).wait()
        blocks = [rx[slot, p].reshape(24, 256) for p in range(PHI)]
        done = filter_lines(blocks, kept_rows, modes, fwd, inv, one, back)
        for p in range(PHI):
            yb[slot, p] = jnp.where(polar[None], done[p].reshape(3, 8, 256), rx[slot, p])

        @pl.when(source)
        def _():
            n = jnp.where(slot == SECOND, DOUBLE, slot)
            here = res.at[pl.ds(3 * n, 3), my_i, mine, :]
            pltpu.make_async_copy(yb.at[slot, phi], here, b_recv.at[n]).start()
            for k in range(1, PHI):
                pltpu.make_async_remote_copy(
                    src_ref=yb.at[slot, others(k)], dst_ref=here, send_sem=b_send, recv_sem=b_recv.at[n],
                    device_id={"phi": others(k)}, device_id_type=MESH,
                ).start()

        straight = helper & (slot == HELPED[-1])

        @pl.when(straight)
        def _():
            for k in range(PHI):
                p = others(k)
                pltpu.make_async_remote_copy(
                    src_ref=yb.at[slot, p], dst_ref=res.at[pl.ds(3 * HELPED[-1], 3), my_i, mine, :],
                    send_sem=b_send, recv_sem=b_recv.at[HELPED[-1]],
                    device_id={"theta": heavy_at, "phi": p}, device_id_type=MESH,
                ).start()

        @pl.when(jnp.logical_not(source | straight))
        def _():
            pltpu.make_async_copy(
                yb.at[slot, phi], rel.at[slot, :, my_i, half_rows, :], rel_recv.at[slot]
            ).start()
            for k in range(1, PHI):
                gather_copy(slot, others(k)).start()

    acc[...] = jnp.zeros((32, 128), F32)
    lane = lax.broadcasted_iota(jnp.int32, (32, 128), 1)

    def finish(n):
        @pl.when(heavy)
        def _():
            whole = res.at[pl.ds(3 * n, 3)]
            pltpu.make_async_copy(whole, whole, b_recv.at[n]).wait()

        @pl.when(light)
        def _():
            part = res.at[pl.ds(3 * n, 3), :, pl.ds(pl.multiple_of(octet * 8, 8), 16), :]
            pltpu.make_async_copy(part, part, b_recv.at[n]).wait()

        total = acc[...]
        for i in range(4):
            v0, v1, v2 = v[0, i], v[1, i], v[2, i]
            r0, r1, r2 = res[3 * n, i], res[3 * n + 1, i], res[3 * n + 2, i]
            terms = (v1 * r2 - v2 * r1, v2 * r0 - v0 * r2, v0 * r1 - v1 * r0)
            for c in range(3):
                summed = jnp.sum(terms[c][:, :128] + terms[c][:, 128:], axis=1, keepdims=True)
                total = jnp.where(lane == 27 * i + 3 * n + c, jnp.broadcast_to(summed, (32, 128)), total)
        acc[...] = total

    def tick(t, _):
        @pl.when(t < STAGES)
        def _():
            step_main(t)

        @pl.when((t >= ELAG) & (t < STAGES + ELAG))
        def _():
            step_edge(t - ELAG)

        for part in range(2):
            first = VIA + ELAG * part

            @pl.when(light & (t >= first) & (t < first + len(FARRED)))
            def _(part=part, first=first):
                pass_on(t - first, part)

        def busy(slot):
            mine = (heavy & member(slot, OWN)) | (light & member(slot, LIGHT_OWN))
            theirs = (helper & member(slot, HELPED)) | (far & (slot >= 0) & (slot < len(FAR_WORK)))
            return mine | theirs

        at = t - jnp.where(helper, HELP, jnp.where(far, FAR, jnp.where(light, LIGHT_BEHIND, BEHIND)))

        slot = at - late

        def work_on(m, _):
            work(jnp.where(m == 1, SECOND, slot))
            return 0

        halves = jnp.where(busy(slot), 1, 0) + jnp.where(heavy & (slot == DOUBLE), 1, 0)
        lax.fori_loop(0, halves, work_on, 0)

        last = at - ELAG - 1

        @pl.when(((helper & (last != HELPED[-1])) | far) & busy(last))
        def _():
            relay(last)

        @pl.when(t >= LAG)
        def _():
            finish(t - LAG)

        return 0

    lax.fori_loop(0, STAGES + LAG, tick, 0)

    def emf_copy(k):
        p = others(k)
        return pltpu.make_async_remote_copy(
            src_ref=acc.at[pl.ds(pl.multiple_of(p // 2 * 8, 8), 8), :], dst_ref=got.at[phi],
            send_sem=emf_send, recv_sem=emf_recv, device_id={"phi": p}, device_id_type=MESH)

    for k in range(1, PHI):
        emf_copy(k).start()
    pltpu.make_async_copy(acc.at[pl.ds(pl.multiple_of(phi // 2 * 8, 8), 8), :], got.at[phi], emf_recv).start()
    pltpu.make_async_copy(got, got, emf_recv).wait()
    summed = got[0]
    for p in range(1, PHI):
        summed = summed + got[p]
    summed = summed * (1.0 / NPHI)
    mean = jnp.where(phi % 2 == 0, summed[:4], summed[4:])
    for i in range(4):
        emf[i] = mean[:, 27 * i : 27 * i + 27]

    seven = got.at[pl.ds(0, 7)]
    drain(seven, emf_send)

    @pl.when(heavy)
    def _():
        keep_copy(1, 0, theta).wait_send()
        keep_copy(1, 1, theta).wait_send()
        for n in range(ACROSS):
            drain(rx.at[0, pl.ds(0, 6)], across_send.at[0, n])
            drain(rx.at[0, pl.ds(0, 2)], across_send.at[1, n])
            drain(vb.at[0, :, pl.ds(0, 3)], via_send.at[0, n])
            drain(vb.at[0, :, pl.ds(0, 1)], via_send.at[1, n])
        drain(rx.at[pl.ds(0, len(OWN) + 1), pl.ds(0, 7)], a_send)
        drain(yb.at[pl.ds(0, len(OWN) + 1), pl.ds(0, 7)], b_send)

    @pl.when(light)
    def _():
        keep_copy(2, 0, theta).wait_send()
        drain(rx.at[pl.ds(0, len(LIGHT_OWN)), pl.ds(0, 7)], a_send)
        drain(yb.at[pl.ds(0, len(LIGHT_OWN)), pl.ds(0, 7)], b_send)
        drain(rx.at[pl.ds(0, len(FAR_WORK))], far_send)

    @pl.when(helper)
    def _():
        drain(yb.at[pl.ds(0, len(HELPED) - 1), pl.ds(0, 7)], b_send)
        drain(yb.at[0], b_send)
        drain(rel.at[pl.ds(0, len(HELPED) - 1)], rel_send)

    @pl.when(far)
    def _():
        drain(yb.at[pl.ds(0, len(FAR_WORK)), pl.ds(0, 7)], b_send)
        drain(rel.at[pl.ds(0, len(FAR_WORK))], rel_send)


def body(test_fields, velocity, kept):
    forward, inverse, singles, singles_back, modes = fourier_constants()
    tables = row_tables()
    hbm, vmem = pl.BlockSpec(memory_space=pltpu.HBM), pl.BlockSpec(memory_space=pltpu.VMEM)
    dma = pltpu.SemaphoreType.DMA
    result, emf = pl.pallas_call(
        kernel,
        out_shape=(
            jax.ShapeDtypeStruct((27, 4, 32, 256), F32),
            jax.ShapeDtypeStruct((4, 4, 27), F32),
        ),
        in_specs=[hbm] * 9,
        out_specs=(vmem, vmem),
        scratch_shapes=[
            pltpu.VMEM((27, 4, 48, 256), F32),
            pltpu.VMEM((3, 4, 32, 256), F32),
            pltpu.VMEM((1, 32), jnp.int32),
            pltpu.VMEM((5, 32, 128), F32),
            pltpu.VMEM(forward.shape, BF16),
            pltpu.VMEM(inverse.shape, BF16),
            pltpu.VMEM(singles.shape, BF16),
            pltpu.VMEM(singles_back.shape, BF16),
            pltpu.VMEM(modes.shape, F32),
            pltpu.VMEM((2, 27, 4, 256), F32),
            pltpu.VMEM((2, 27, 4, 256), F32),
            pltpu.VMEM((27, 32, 256), F32),
            pltpu.VMEM((3, 4, 32, 256), F32),
            pltpu.SMEM((2, 4), F32),
            pltpu.VMEM((3, 32, 128), F32),
            pltpu.VMEM((32, 128), F32),
            pltpu.VMEM((27, 4, 32, 256), F32),
            pltpu.VMEM((STAGES + 1, PHI, 3, 8, 256), F32),
            pltpu.VMEM((STAGES + 1, PHI, 3, 8, 256), F32),
            pltpu.VMEM((STAGES, 3, 4, 16, 256), F32),
            pltpu.VMEM((len(FARRED), 3, 4, 16, 256), F32),
            pltpu.VMEM((32, 128), F32),
            pltpu.VMEM((PHI, 8, 128), F32),
            dma((10,)),
            dma((2, len(PIECES))),
            dma((2, len(PIECES))),
            dma((STAGES,)),
            dma((STAGES,)),
            dma((2,)),
            dma((2,)),
            dma,
            dma((2, ACROSS)),
            dma((2, ACROSS)),
            dma((2, len(FARRED))),
            dma,
            dma((STAGES + 1,)),
            dma,
            dma((STAGES,)),
            dma,
            dma((STAGES,)),
            dma,
            dma,
        ],
        compiler_params=pltpu.CompilerParams(
            collective_id=0, has_side_effects=True, vmem_limit_bytes=40 * 2**20
        ),
        name="substep",
    )(
        *(
            pltpu.with_memory_space_constraint(jnp.asarray(a), pltpu.HBM)
            for a in (
                test_fields, velocity, kept.reshape(1, 32), tables, forward, inverse, singles, singles_back, modes,
            )
        )
    )
    return result, jnp.transpose(emf, (2, 0, 1))


def solution(mesh):
    return jax.shard_map(
        body,
        mesh=mesh,
        in_specs=(P(None, "row", "theta", "phi"), P(None, "row", "theta", "phi"), P("theta")),
        out_specs=(P(None, "row", "theta", "phi"), P(None, "row", ("theta", "phi"))),
        check_vma=False,
    )
```
